256 devices in a mesh: group: 16 (over x_lo, z), blk: 16 (over y, x_hi, core).
Axes of the slice: x: 4 (x_hi: 2, x_lo: 2; x = x_hi * 2 + x_lo), y: 4, z: 8, core: 2. Of those that a mesh axis runs over, the one named last changes fastest.
Arguments:
- student: bfloat16 [16384, 1024], P('group'), may hold values from -8 to 8
- teacher: bfloat16 [16384, 1024], P('group'), may hold values from -8 to 8
Outputs:
- student_grad: float32 [16384, 1024], P(('group', 'blk'))
The draws below stay inside these ranges and needn't reach their ends.
All inputs are finite; a program needn't handle non-finite values.
Results may differ from the reference program's by a relative error of at most 0.0008.
Values may be sent and summed in bfloat16 or wider, within the bound.
A program may use at most 64 MiB of HBM per device.

```python
import jax
import jax.numpy as jnp
from jax import lax

D = 1024
TOKENS = 16384


def shared_layout(key):
    centre_key, scale_key = jax.random.split(key)
    centres = jax.random.normal(centre_key, (64, 16), jnp.float32)
    feature_scale = jax.random.normal(scale_key, (D,), jnp.float32)
    return (centres, feature_scale)


def assemble(centres, feature_scale, member, centre_scale, jitter, noise):
    coefs = centre_scale * jnp.take(centres, member, axis=0) + jitter
    feature_group = jnp.arange(D) % 16
    spread = jnp.take(coefs, feature_group, axis=1)
    values = spread * feature_scale[None, :] + noise
    return jnp.clip(values, -8.0, 8.0).astype(jnp.bfloat16)


def draw_student(key, part):
    centres, feature_scale = shared_layout(key)
    key = jax.random.fold_in(key, 11)
    pick_key, jitter_key, noise_key = jax.random.split(key, 3)
    member = jax.random.randint(pick_key, (TOKENS,), 0, 64)
    jitter = 0.25 * jax.random.normal(jitter_key, (TOKENS, 16), jnp.float32)
    noise = 0.3 * jax.random.normal(noise_key, (TOKENS, D), jnp.float32)
    return assemble(centres, feature_scale, member, 1.0, jitter, noise)


def draw_teacher(key, part):
    centres, feature_scale = shared_layout(key)
    key = jax.random.fold_in(key, 13)
    pick_key, jitter_key, noise_key = jax.random.split(key, 3)
    member = jax.random.randint(pick_key, (TOKENS,), 0, 64)
    jitter = 0.3 * jax.random.normal(jitter_key, (TOKENS, 16), jnp.float32)
    noise = 0.35 * jax.random.normal(noise_key, (TOKENS, D), jnp.float32)
    return assemble(centres, feature_scale, member, 1.15, jitter, noise)


def setup_inputs(seed: int = 0) -> dict:
    streams_of = jax.random.split(jax.random.key(seed), 3)
    return {
        "student": draw_student(jax.random.fold_in(streams_of[2], 71), 0),
        "teacher": draw_teacher(jax.random.fold_in(streams_of[2], 71), 0),
    }


SCALE_FACTORS = (0.5, 1.0, 2.0, 4.0, 8.0)


def kernel_weights(distance, feature_width):
    summed = jnp.zeros(distance.shape, jnp.float32)
    for factor in SCALE_FACTORS:
        summed = summed + (2.0 / factor) * jnp.exp(-distance / (feature_width * factor))
    return summed.astype(jnp.bfloat16)


def squares(values):
    wide = values.astype(jnp.float32)
    return jnp.sum(wide * wide, axis=1)


def cross(left, right):
    return lax.dot_general(left, right, (((1,), (1,)), ((), ())), preferred_element_type=jnp.float32)


def pair_terms(row_block, row_norm, student_cols, teacher_cols):
    feature_width = row_block.shape[1]
    near_dist = (row_norm[:, None] + squares(student_cols)[None, :]) - 2.0 * cross(row_block, student_cols)
    far_dist = (row_norm[:, None] + squares(teacher_cols)[None, :]) - 2.0 * cross(row_block, teacher_cols)
    near_weights = kernel_weights(near_dist, feature_width)
    far_weights = kernel_weights(far_dist, feature_width)
    pulled = jnp.dot(near_weights, student_cols, preferred_element_type=jnp.float32)
    pulled = pulled - jnp.dot(far_weights, teacher_cols, preferred_element_type=jnp.float32)
    mass_diff = jnp.sum(near_weights.astype(jnp.float32), axis=1) - jnp.sum(far_weights.astype(jnp.float32), axis=1)
    return pulled - mass_diff[:, None] * row_block.astype(jnp.float32)


def reference(student, teacher):
    block_rows = min(512, TOKENS)
    blocks = student.reshape(TOKENS // block_rows, block_rows, D)

    def one_block(row_block):
        return pair_terms(row_block, squares(row_block), student, teacher)

    pulled = lax.map(one_block, blocks).reshape(TOKENS, D)
    return pulled / jnp.float32(TOKENS)
```

```python
import functools
import math

import jax
import jax.numpy as jnp
from jax import lax
from jax.experimental import pallas as pl
from jax.experimental.pallas import tpu as pltpu
from jax.sharding import PartitionSpec as P

X_HI = 2
X_LO = 2
CORES = 2
X = X_HI * X_LO
WIDEST = 8.0

LOW = 0.25 * 2.0 ** -0.125
MID = 0.5 * 2.0 ** -0.25
HIGH = 2.0 ** -0.5


def kernel(student, teacher, out, rows, cols, acc, norm, mass, mate, stage, landed,
           load_sem, z_send, z_recv, x_send, x_recv, mate_send, mate_recv, red_send, red_recv,
           *, groups, blks):
    nz = groups // X_LO
    ny = blks // (X_HI * CORES)
    local_rows, width = rows.shape
    part_rows = cols.shape[3]
    share_rows = local_rows // blks
    block_rows = X_HI * CORES * share_rows
    half_nz = nz // 2

    group = lax.axis_index("group")
    blk = lax.axis_index("blk")
    x_lo, z = group // nz, lax.rem(group, nz)
    y, x_hi, core = blk // (X_HI * CORES), lax.rem(blk // CORES, X_HI), lax.rem(blk, CORES)
    x = x_hi * X_LO + x_lo

    def at_z(step):
        return {"group": x_lo * nz + lax.rem(z + step + nz, nz), "blk": blk}

    def at_x(step):
        to = lax.rem(x + step + X, X)
        return {
            "group": lax.rem(to, X_LO) * nz + z,
            "blk": (y * X_HI + to // X_LO) * CORES + core,
        }

    def at_owner(dy, dx):
        to_y, to_x = lax.rem(y + dy, ny), lax.rem(x_hi + dx, X_HI)
        return {"group": group, "blk": (to_y * X_HI + to_x) * CORES + core}

    sibling = {"group": group, "blk": blk + 1 - 2 * core}
    owners = [(dy, dx) for dy in range(ny) for dx in range(X_HI)]
    sources = (student, teacher)

    def own_part(kind, part):
        quarter = lax.rem(x + part, X)
        start = ((y * X + quarter) * CORES + core) * part_rows
        return sources[kind].at[pl.ds(pl.multiple_of(start, part_rows), part_rows)]

    def slot_of(way, dist):
        if dist == 0:
            return 0
        if dist == half_nz:
            return nz - 1
        return dist if way == 0 else half_nz - 1 + dist

    def z_copy(way, dist, kind, part):
        src = own_part(kind, part) if dist == 1 else cols.at[slot_of(way, dist - 1), kind, part]
        return pltpu.make_async_remote_copy(
            src_ref=src,
            dst_ref=cols.at[slot_of(way, dist), kind, part],
            send_sem=z_send.at[way, dist - 1, kind, part],
            recv_sem=z_recv.at[way, dist - 1, kind, part],
            device_id=at_z(1 if way == 0 else -1),
            device_id_type=pl.DeviceIdType.MESH,
        )

    def x_copy(slot, kind, part):
        src = own_part(kind, part) if slot == 0 else cols.at[slot, kind, part]
        return pltpu.make_async_remote_copy(
            src_ref=src,
            dst_ref=cols.at[slot, kind, 3 - part],
            send_sem=x_send.at[slot, kind, part],
            recv_sem=x_recv.at[slot, kind, part],
            device_id=at_x(-1 if part == 0 else 1),
            device_id_type=pl.DeviceIdType.MESH,
        )

    def block_at(to_y):
        return pl.ds(pl.multiple_of(to_y * block_rows, block_rows), block_rows)

    def share_at(dy, dx, of_core):
        owner = (lax.rem(y + dy, ny) * X_HI + lax.rem(x_hi + dx, X_HI)) * CORES + of_core
        return pl.ds(pl.multiple_of(owner * share_rows, share_rows), share_rows)

    def mate_copy(dy, dx):
        return pltpu.make_async_remote_copy(
            src_ref=acc.at[share_at(dy, dx, 1 - core)],
            dst_ref=mate.at[dy, dx],
            send_sem=mate_send.at[dy, dx],
            recv_sem=mate_recv.at[dy, dx],
            device_id=sibling,
            device_id_type=pl.DeviceIdType.MESH,
        )

    def owner_copy(dy, dx):
        return pltpu.make_async_remote_copy(
            src_ref=stage.at[dy, dx],
            dst_ref=landed.at[dy, dx],
            send_sem=red_send.at[dy, dx],
            recv_sem=red_recv.at[dy, dx],
            device_id=at_owner(dy, dx),
            device_id_type=pl.DeviceIdType.MESH,
        )

    subs = [(kind, part) for kind in range(2) for part in range(2)]
    loads = [pltpu.make_async_copy(student, rows, load_sem.at[0])]
    for i, (kind, part) in enumerate(subs):
        loads.append(
            pltpu.make_async_copy(own_part(kind, part), cols.at[0, kind, part], load_sem.at[1 + i])
        )
    for copy in loads:
        copy.start()

    barrier = pltpu.get_barrier_semaphore()
    partners = [at_z(1), at_z(-1), at_x(1), at_x(-1), sibling]
    partners += [at_owner(dy, dx) for dy, dx in owners if (dy, dx) != (0, 0)]
    for partner in partners:
        pl.semaphore_signal(barrier, inc=1, device_id=partner, device_id_type=pl.DeviceIdType.MESH)
    pl.semaphore_wait(barrier, len(partners))

    sent = []

    def send(copy):
        copy.start()
        sent.append(copy)

    for kind, part in subs:
        send(z_copy(0, 1, kind, part))
        send(z_copy(1, 1, kind, part))
        send(x_copy(0, kind, part))

    def pass_on(way, dist, kind, part):
        z_copy(way, dist, kind, part).wait_recv()
        if dist + 1 < half_nz or (dist + 1 == half_nz and part == way):
            send(z_copy(way, dist + 1, kind, part))
        send(x_copy(slot_of(way, dist), kind, part))

    rate = math.log2(math.e) / (WIDEST * width)

    loads[0].wait()

    @pl.loop(0, ny)
    def _(i):
        wide = rows[block_at(i), :].astype(jnp.float32)
        total = jnp.sum(wide * wide, axis=1, keepdims=True)
        norm[block_at(i), :] = jnp.broadcast_to(0.125 - rate * total, (block_rows, 128))

    def columns(slot):
        return cols[slot].reshape(-1, width)

    def column_norm(slot):
        wide = columns(slot).astype(jnp.float32)
        squared = wide * wide
        folded = squared[:, :128]
        for k in range(128, width, 128):
            folded = folded + squared[:, k : k + 128]
        return -rate * jnp.sum(folded.T, axis=0, keepdims=True)

    def weigh(slot, col_norm, where, first):
        col = columns(slot)
        count = col.shape[0]
        inner = lax.dot_general(
            rows[where, :], col, (((1,), (1,)), ((), ())), preferred_element_type=jnp.float32
        )
        row_norm = jnp.concatenate([norm[where, :]] * (count // 128), axis=1)
        f = jnp.exp2(inner * (2.0 * rate) + (row_norm + col_norm))
        f2 = f * f
        f4 = f2 * f2
        f8 = f4 * f4
        summed = f * (LOW + f * (MID + f2 * (HIGH + f4 * (1.0 + f8))))
        near = summed[:, : count // 2]
        far = -summed[:, count // 2 :]
        weights = jnp.concatenate([near, far], axis=1).astype(jnp.bfloat16)
        wide = weights.astype(jnp.float32)
        folded = wide[:, :128]
        for k in range(128, count, 128):
            folded = folded + wide[:, k : k + 128]
        pulled = jnp.dot(weights, col, preferred_element_type=jnp.float32)
        if first:
            mass[where, :] = folded
            acc[where, :] = pulled
        else:
            mass[where, :] += folded
            acc[where, :] += pulled

    def wait_x(slot):
        for kind, part in subs:
            x_copy(slot, kind, part).wait_recv()

    def use(slot, first=False):
        wait_x(slot)
        col_norm = column_norm(slot)

        @pl.loop(0, ny)
        def _(i):
            weigh(slot, col_norm, block_at(i), first)

    def arrive(dist, picked):
        for kind, part in picked:
            for way in range(2):
                if dist < half_nz or part == way:
                    pass_on(way, dist, kind, part)

    arrive(1, subs[:2])
    for copy in loads[1:]:
        copy.wait()
    use(0, first=True)
    arrive(1, subs[2:])
    for dist in range(2, half_nz):
        arrive(dist, subs[:2])
        use(slot_of(0, dist - 1))
        arrive(dist, subs[2:3])
        use(slot_of(1, dist - 1))
        arrive(dist, subs[3:])
    arrive(half_nz, subs)
    use(slot_of(0, half_nz - 1))
    use(slot_of(1, half_nz - 1))

    last = nz - 1
    wait_x(last)
    last_norm = column_norm(last)

    def hand_over(dy):
        for dx in range(X_HI):
            mate_copy(dy, dx).wait_recv()
            total = acc[share_at(dy, dx, core), :] + mate[dy, dx]
            if (dy, dx) == (0, 0):
                out[...] = total
            else:
                stage[dy, dx] = total.astype(jnp.bfloat16)
                send(owner_copy(dy, dx))

    order = list(range(1, ny)) + [0]
    for i, dy in enumerate(order):
        where = block_at(lax.rem(y + dy, ny))
        weigh(last, last_norm, where, False)
        diff = jnp.sum(mass[where, :], axis=1, keepdims=True)
        acc[where, :] -= diff * rows[where, :].astype(jnp.float32)
        for dx in range(X_HI):
            send(mate_copy(dy, dx))
        if i > 0:
            hand_over(order[i - 1])
    hand_over(order[-1])

    total = out[...]
    for dy, dx in owners:
        if (dy, dx) != (0, 0):
            owner_copy(dy, dx).wait_recv()
            total = total + landed[dy, dx].astype(jnp.float32)
    out[...] = total * (1.0 / (groups * local_rows))
    for copy in sent:
        copy.wait_send()


def local(student, teacher):
    groups, blks = lax.axis_size("group"), lax.axis_size("blk")
    local_rows, width = student.shape
    nz, ny = groups // X_LO, blks // (X_HI * CORES)
    share_rows = local_rows // blks
    part_rows = local_rows // (ny * X * CORES)
    dma = pltpu.SemaphoreType.DMA
    pairs = groups * local_rows * 2 * groups * local_rows // (groups * blks)
    return pl.pallas_call(
        functools.partial(kernel, groups=groups, blks=blks),
        out_shape=jax.ShapeDtypeStruct((share_rows, width), jnp.float32),
        in_specs=[pl.BlockSpec(memory_space=pl.ANY)] * 2,
        out_specs=pl.BlockSpec(memory_space=pltpu.VMEM),
        scratch_shapes=[
            pltpu.VMEM((local_rows, width), jnp.bfloat16),
            pltpu.VMEM((nz, 2, 4, part_rows, width), jnp.bfloat16),
            pltpu.VMEM((local_rows, width), jnp.float32),
            pltpu.VMEM((local_rows, 128), jnp.float32),
            pltpu.VMEM((local_rows, 128), jnp.float32),
            pltpu.VMEM((ny, X_HI, share_rows, width), jnp.float32),
            pltpu.VMEM((ny, X_HI, share_rows, width), jnp.bfloat16),
            pltpu.VMEM((ny, X_HI, share_rows, width), jnp.bfloat16),
            dma((5,)),
            dma((2, nz // 2, 2, 2)),
            dma((2, nz // 2, 2, 2)),
            dma((nz, 2, 2)),
            dma((nz, 2, 2)),
            dma((ny, X_HI)),
            dma((ny, X_HI)),
            dma((ny, X_HI)),
            dma((ny, X_HI)),
        ],
        compiler_params=pltpu.CompilerParams(
            collective_id=0, has_side_effects=True, vmem_limit_bytes=48 * 1024 * 1024
        ),
        cost_estimate=pl.CostEstimate(
            flops=4 * pairs * width, bytes_accessed=8 * 1024 * 1024, transcendentals=pairs
        ),
    )(student, teacher)


def solution(mesh):
    in_specs = (P("group", None), P("group", None))
    out_specs = P(("group", "blk"), None)
    return jax.shard_map(local, mesh=mesh, in_specs=in_specs, out_specs=out_specs, check_vma=False)
```

```python
import functools
import math

import jax
import jax.numpy as jnp
from jax import lax
from jax.experimental import pallas as pl
from jax.experimental.pallas import tpu as pltpu
from jax.sharding import PartitionSpec as P

X_HI = 2
X_LO = 2
CORES = 2
X = X_HI * X_LO
WIDEST = 8.0

LOW = 0.25 * 2.0 ** -0.125
MID = 0.5 * 2.0 ** -0.25
HIGH = 2.0 ** -0.5


def kernel(student, teacher, out, rows, cols, acc, norm, mass, mate, stage, landed,
           load_sem, z_send, z_recv, x_send, x_recv, mate_send, mate_recv, red_send, red_recv,
           *, groups, blks):
    nz = groups // X_LO
    ny = blks // (X_HI * CORES)
    local_rows, width = rows.shape
    part_rows = cols.shape[3]
    share_rows = local_rows // blks
    block_rows = X_HI * CORES * share_rows
    half_nz = nz // 2

    group = lax.axis_index("group")
    blk = lax.axis_index("blk")
    x_lo, z = group // nz, lax.rem(group, nz)
    y, x_hi, core = blk // (X_HI * CORES), lax.rem(blk // CORES, X_HI), lax.rem(blk, CORES)
    x = x_hi * X_LO + x_lo

    def at_z(step):
        return {"group": x_lo * nz + lax.rem(z + step + nz, nz), "blk": blk}

    def at_x(step):
        to = lax.rem(x + step + X, X)
        return {
            "group": lax.rem(to, X_LO) * nz + z,
            "blk": (y * X_HI + to // X_LO) * CORES + core,
        }

    def at_owner(dy, dx):
        to_y, to_x = lax.rem(y + dy, ny), lax.rem(x_hi + dx, X_HI)
        return {"group": group, "blk": (to_y * X_HI + to_x) * CORES + core}

    sibling = {"group": group, "blk": blk + 1 - 2 * core}
    owners = [(dy, dx) for dy in range(ny) for dx in range(X_HI)]
    sources = (student, teacher)

    def own_part(kind, part):
        quarter = lax.rem(x + part, X)
        start = ((y * X + quarter) * CORES + core) * part_rows
        return sources[kind].at[pl.ds(pl.multiple_of(start, part_rows), part_rows)]

    def slot_of(way, dist):
        if dist == 0:
            return 0
        if dist == half_nz:
            return nz - 1
        return 2 * dist - 1 + way

    def z_copy(way, dist, kind, part):
        src = own_part(kind, part) if dist == 1 else cols.at[slot_of(way, dist - 1), kind, part]
        return pltpu.make_async_remote_copy(
            src_ref=src,
            dst_ref=cols.at[slot_of(way, dist), kind, part],
            send_sem=z_send.at[way, dist - 1, kind, part],
            recv_sem=z_recv.at[way, dist - 1, kind, part],
            device_id=at_z(1 if way == 0 else -1),
            device_id_type=pl.DeviceIdType.MESH,
        )

    def x_copy(slot, kind, part):
        src = own_part(kind, part) if slot == 0 else cols.at[slot, kind, part]
        return pltpu.make_async_remote_copy(
            src_ref=src,
            dst_ref=cols.at[slot, kind, 3 - part],
            send_sem=x_send.at[slot, kind, part],
            recv_sem=x_recv.at[slot, kind, part],
            device_id=at_x(-1 if part == 0 else 1),
            device_id_type=pl.DeviceIdType.MESH,
        )

    def block_at(to_y):
        return pl.ds(pl.multiple_of(to_y * block_rows, block_rows), block_rows)

    def share_at(dy, dx, of_core):
        owner = (lax.rem(y + dy, ny) * X_HI + lax.rem(x_hi + dx, X_HI)) * CORES + of_core
        return pl.ds(pl.multiple_of(owner * share_rows, share_rows), share_rows)

    def mate_copy(dy, dx):
        return pltpu.make_async_remote_copy(
            src_ref=acc.at[share_at(dy, dx, 1 - core)],
            dst_ref=mate.at[dy, dx],
            send_sem=mate_send.at[dy, dx],
            recv_sem=mate_recv.at[dy, dx],
            device_id=sibling,
            device_id_type=pl.DeviceIdType.MESH,
        )

    def owner_copy(dy, dx):
        return pltpu.make_async_remote_copy(
            src_ref=stage.at[dy, dx],
            dst_ref=landed.at[dy, dx],
            send_sem=red_send.at[dy, dx],
            recv_sem=red_recv.at[dy, dx],
            device_id=at_owner(dy, dx),
            device_id_type=pl.DeviceIdType.MESH,
        )

    subs = [(kind, part) for kind in range(2) for part in range(2)]
    loads = [pltpu.make_async_copy(student, rows, load_sem.at[0])]
    for i, (kind, part) in enumerate(subs):
        loads.append(
            pltpu.make_async_copy(own_part(kind, part), cols.at[0, kind, part], load_sem.at[1 + i])
        )
    for copy in loads:
        copy.start()

    barrier = pltpu.get_barrier_semaphore()
    partners = [at_z(1), at_z(-1), at_x(1), at_x(-1), sibling]
    partners += [at_owner(dy, dx) for dy, dx in owners if (dy, dx) != (0, 0)]
    for partner in partners:
        pl.semaphore_signal(barrier, inc=1, device_id=partner, device_id_type=pl.DeviceIdType.MESH)
    pl.semaphore_wait(barrier, len(partners))

    sent = []

    def send(copy):
        copy.start()
        sent.append(copy)

    def sub_of(way, i):
        return i // 2, (i + way) % 2

    for i in range(4):
        for way in range(2):
            send(z_copy(way, 1, *sub_of(way, i)))
        send(x_copy(0, *subs[i]))

    def pass_on(way, dist, kind, part):
        z_copy(way, dist, kind, part).wait_recv()
        if dist + 1 < half_nz or (dist + 1 == half_nz and part == way):
            send(z_copy(way, dist + 1, kind, part))
        send(x_copy(slot_of(way, dist), kind, part))

    rate = math.log2(math.e) / (WIDEST * width)

    loads[0].wait()

    @pl.loop(0, ny)
    def _(i):
        wide = rows[block_at(i), :].astype(jnp.float32)
        total = jnp.sum(wide * wide, axis=1, keepdims=True)
        norm[block_at(i), :] = jnp.broadcast_to(0.125 - rate * total, (block_rows, 128))

    def columns(slot, count):
        return cols[slot : slot + count].reshape(-1, width)

    def column_norm(slot, count):
        wide = columns(slot, count).astype(jnp.float32)
        squared = wide * wide
        folded = squared[:, :128]
        for k in range(128, width, 128):
            folded = folded + squared[:, k : k + 128]
        return -rate * jnp.sum(folded.T, axis=0, keepdims=True)

    def weigh(slot, count, col_norm, where, first=False):
        col = columns(slot, count)
        inner = lax.dot_general(
            rows[where, :], col, (((1,), (1,)), ((), ())), preferred_element_type=jnp.float32
        )
        lanes = 4 * part_rows
        row_norm = norm[where, :]
        weights = []
        folded = None
        for k in range(2 * count):
            span = slice(k * lanes, (k + 1) * lanes)
            f = jnp.exp2(inner[:, span] * (2.0 * rate) + (row_norm + col_norm[:, span]))
            f2 = f * f
            f4 = f2 * f2
            f8 = f4 * f4
            summed = f * (LOW + f * (MID + f2 * (HIGH + f4 * (1.0 + f8))))
            weight = (summed if k % 2 == 0 else -summed).astype(jnp.bfloat16)
            weights.append(weight)
            wide = weight.astype(jnp.float32)
            folded = wide if folded is None else folded + wide
        pulled = jnp.dot(
            jnp.concatenate(weights, axis=1), col, preferred_element_type=jnp.float32
        )
        if first:
            mass[where, :] = folded
            acc[where, :] = pulled
        else:
            mass[where, :] += folded
            acc[where, :] += pulled

    def wait_x(slot):
        for kind, part in subs:
            x_copy(slot, kind, part).wait_recv()

    def half_rows(i):
        return slice(i * local_rows // 2, (i + 1) * local_rows // 2)

    def arrive(dist, i):
        for way in range(2):
            pass_on(way, dist, *sub_of(way, i))

    for copy in loads[1:]:
        copy.wait()
    arrive(1, 0)
    arrive(1, 1)
    wait_x(0)
    col_norm = column_norm(0, 1)
    for i in range(2):
        weigh(0, 1, col_norm, half_rows(i), first=True)
    arrive(1, 2)
    arrive(1, 3)
    for dist in range(2, half_nz):
        slot = slot_of(0, dist - 1)
        arrive(dist, 0)
        arrive(dist, 1)
        wait_x(slot)
        wait_x(slot + 1)
        col_norm = column_norm(slot, 2)
        weigh(slot, 2, col_norm, half_rows(0))
        arrive(dist, 2)
        weigh(slot, 2, col_norm, half_rows(1))
        arrive(dist, 3)
    for i in (0, 2):
        arrive(half_nz, i)
    slot = slot_of(0, half_nz - 1)
    wait_x(slot)
    wait_x(slot + 1)
    col_norm = column_norm(slot, 2)
    for i in range(2):
        weigh(slot, 2, col_norm, half_rows(i))

    last = nz - 1
    wait_x(last)
    last_norm = column_norm(last, 1)
    gathered = sent
    sent = []

    def hand_over(dy):
        for dx in range(X_HI):
            mate_copy(dy, dx).wait_recv()
            total = acc[share_at(dy, dx, core), :] + mate[dy, dx]
            if (dy, dx) == (0, 0):
                out[...] = total
            else:
                stage[dy, dx] = total.astype(jnp.bfloat16)
                send(owner_copy(dy, dx))

    order = [2, 1, 3, 0] if ny == 4 else list(range(ny))
    for i, dy in enumerate(order):
        where = block_at(lax.rem(y + dy, ny))
        weigh(last, 1, last_norm, where)
        diff = jnp.sum(mass[where, :], axis=1, keepdims=True)
        acc[where, :] -= diff * rows[where, :].astype(jnp.float32)
        for dx in range(X_HI):
            send(mate_copy(dy, dx))
        if i > 0:
            hand_over(order[i - 1])
    hand_over(order[-1])

    for copy in gathered:
        copy.wait_send()
    total = out[...]
    for dy, dx in owners:
        if (dy, dx) != (0, 0):
            owner_copy(dy, dx).wait_recv()
            total = total + landed[dy, dx].astype(jnp.float32)
    out[...] = total * (1.0 / (groups * local_rows))
    for copy in sent:
        copy.wait_send()


def local(student, teacher):
    groups, blks = lax.axis_size("group"), lax.axis_size("blk")
    local_rows, width = student.shape
    nz, ny = groups // X_LO, blks // (X_HI * CORES)
    share_rows = local_rows // blks
    part_rows = local_rows // (ny * X * CORES)
    dma = pltpu.SemaphoreType.DMA
    pairs = groups * local_rows * 2 * groups * local_rows // (groups * blks)
    return pl.pallas_call(
        functools.partial(kernel, groups=groups, blks=blks),
        out_shape=jax.ShapeDtypeStruct((share_rows, width), jnp.float32),
        in_specs=[pl.BlockSpec(memory_space=pl.ANY)] * 2,
        out_specs=pl.BlockSpec(memory_space=pltpu.VMEM),
        scratch_shapes=[
            pltpu.VMEM((local_rows, width), jnp.bfloat16),
            pltpu.VMEM((nz, 2, 4, part_rows, width), jnp.bfloat16),
            pltpu.VMEM((local_rows, width), jnp.float32),
            pltpu.VMEM((local_rows, 128), jnp.float32),
            pltpu.VMEM((local_rows, 128), jnp.float32),
            pltpu.VMEM((ny, X_HI, share_rows, width), jnp.float32),
            pltpu.VMEM((ny, X_HI, share_rows, width), jnp.bfloat16),
            pltpu.VMEM((ny, X_HI, share_rows, width), jnp.bfloat16),
            dma((5,)),
            dma((2, nz // 2, 2, 2)),
            dma((2, nz // 2, 2, 2)),
            dma((nz, 2, 2)),
            dma((nz, 2, 2)),
            dma((ny, X_HI)),
            dma((ny, X_HI)),
            dma((ny, X_HI)),
            dma((ny, X_HI)),
        ],
        compiler_params=pltpu.CompilerParams(
            collective_id=0, has_side_effects=True, vmem_limit_bytes=60 * 1024 * 1024
        ),
        cost_estimate=pl.CostEstimate(
            flops=4 * pairs * width, bytes_accessed=8 * 1024 * 1024, transcendentals=pairs
        ),
    )(student, teacher)


def solution(mesh):
    in_specs = (P("group", None), P("group", None))
    out_specs = P(("group", "blk"), None)
    return jax.shard_map(local, mesh=mesh, in_specs=in_specs, out_specs=out_specs, check_vma=False)
```

```python
import functools
import math

import jax
import jax.numpy as jnp
from jax import lax
from jax.experimental import pallas as pl
from jax.experimental.pallas import tpu as pltpu
from jax.sharding import PartitionSpec as P

X_HI = 2
X_LO = 2
CORES = 2
X = X_HI * X_LO
WIDEST = 8.0

LOW = 0.25 * 2.0 ** -0.125
MID = 0.5 * 2.0 ** -0.25
HIGH = 2.0 ** -0.5


def kernel(student, teacher, out, rows, cols, acc, norm, mass, stage, landed,
           row_sem, load_sem, first_send, first_recv, split_send, z_send, z_recv, x_send, x_recv, mate_send, mate_recv,
           red_send, red_recv, *, groups, blks):
    nz = groups // X_LO
    ny = blks // (X_HI * CORES)
    width = rows.shape[1]
    part_rows = cols.shape[5]
    share_rows = rows.shape[0] // (ny * X_HI)
    half_nz = nz // 2
    last = nz - 1

    group = lax.axis_index("group")
    blk = lax.axis_index("blk")
    x_lo, z = group // nz, lax.rem(group, nz)
    y, x_hi, core = blk // (X_HI * CORES), lax.rem(blk // CORES, X_HI), lax.rem(blk, CORES)
    x = x_hi * X_LO + x_lo

    def at_z(step):
        return {"group": x_lo * nz + lax.rem(z + step + nz, nz), "blk": blk}

    def at_x(step):
        to = lax.rem(x + step + X, X)
        return {
            "group": lax.rem(to, X_LO) * nz + z,
            "blk": (y * X_HI + to // X_LO) * CORES + core,
        }

    def share_of(dy, dx):
        return (lax.rem(y + dy, ny) * X_HI + lax.rem(x_hi + dx, X_HI)) * CORES + core

    def at_owner(dy, dx):
        return {"group": group, "blk": share_of(dy, dx)}

    sibling = {"group": group, "blk": blk + 1 - 2 * core}
    owners = [(dy, dx) for dy in ([2, 1, 3, 0] if ny == 4 else range(ny - 1, -1, -1)) for dx in (1, 0)]
    sources = (student, teacher)

    def remote(src, dst, send_sem, recv_sem, to):
        return pltpu.make_async_remote_copy(
            src_ref=src,
            dst_ref=dst,
            send_sem=send_sem,
            recv_sem=recv_sem,
            device_id=to,
            device_id_type=pl.DeviceIdType.MESH,
        )

    def own_part(kind, part, of_core):
        quarter = lax.rem(x + part, X)
        start = ((y * X + quarter) * CORES + of_core) * part_rows
        return sources[kind].at[pl.ds(pl.multiple_of(start, part_rows), part_rows)]

    def slot_of(way, dist):
        if dist == 0:
            return 0
        if dist == half_nz:
            return last
        return 2 * dist - 1 + way

    def z_copy(way, dist, part):
        at = (way, dist - 1, part)
        return remote(
            cols.at[slot_of(way, dist - 1), 0, 0, part],
            cols.at[slot_of(way, dist), 0, 0, part],
            z_send.at[at],
            z_recv.at[at],
            at_z(1 if way == 0 else -1),
        )

    def z_first(way, part, kind):
        at = (way, part, kind)
        return remote(
            own_part(kind, part, core),
            cols.at[slot_of(way, 1), 0, 0, part, kind],
            first_send.at[at],
            first_recv.at[at],
            at_z(1 if way == 0 else -1),
        )

    def x_copy(slot, part, kind=None):
        src, dst = cols.at[slot, 0, 0, part], cols.at[slot, 1, 0, 1 - part]
        send_sem = x_send.at[slot, part]
        if kind is not None:
            src = own_part(kind, part, core) if slot == 0 else src.at[kind]
            dst, send_sem = dst.at[kind], split_send.at[slot, part, kind]
        return remote(src, dst, send_sem, x_recv.at[slot, part], at_x(-1 if part == 0 else 1))

    def mate_copy(slot, half, part):
        at = (slot, half, part)
        return remote(
            cols.at[slot, half, 0, part],
            cols.at[slot, half, 1, part],
            mate_send.at[at],
            mate_recv.at[at],
            sibling,
        )

    def owner_copy(i):
        return remote(stage.at[i], landed.at[i], red_send.at[i], red_recv.at[i], at_owner(*owners[i]))

    subs = [(kind, part) for kind in range(2) for part in range(2)]

    barrier = pltpu.get_barrier_semaphore()
    partners = [at_z(1), at_z(-1), at_x(1), at_x(-1), sibling]
    partners += [at_owner(dy, dx) for dy, dx in owners if (dy, dx) != (0, 0)]
    for partner in partners:
        pl.semaphore_signal(barrier, inc=1, device_id=partner, device_id_type=pl.DeviceIdType.MESH)

    row_loads = []
    for i, (dy, dx) in enumerate(owners):
        start = pl.multiple_of(share_of(dy, dx) * share_rows, share_rows)
        row_loads.append(
            pltpu.make_async_copy(
                student.at[pl.ds(start, share_rows)],
                rows.at[pl.ds(i * share_rows, share_rows)],
                row_sem.at[i],
            )
        )
    col_loads = []
    for who in range(2):
        of_core = core if who == 0 else 1 - core
        for kind, part in subs:
            col_loads.append(
                pltpu.make_async_copy(
                    own_part(kind, part, of_core),
                    cols.at[0, 0, who, part, kind],
                    load_sem.at[who, kind, part],
                )
            )
    for copy in row_loads + col_loads:
        copy.start()
    pl.semaphore_wait(barrier, len(partners))

    gathered = []

    def send(copy, sent=gathered):
        copy.start()
        sent.append(copy)

    for i in range(2):
        for kind in range(2):
            for way in range(2):
                send(z_first(way, (i + way) % 2, kind))
            send(x_copy(0, i, kind))

    rate = math.log2(math.e) / (WIDEST * width)
    lanes = 4 * part_rows
    lane = lax.broadcasted_iota(jnp.int32, (1, lanes), 1)
    sign = jnp.where(lax.rem(lane, 2 * part_rows) < part_rows, 1.0, -1.0)

    for copy in row_loads:
        copy.wait()
    for copy in col_loads:
        copy.wait()
    wide_rows = rows[...].astype(jnp.float32)
    row_squares = jnp.sum(wide_rows * wide_rows, axis=1, keepdims=True)
    norm[...] = jnp.broadcast_to(0.125 - rate * row_squares, norm.shape)

    def weigh(read, where):
        col = read().reshape(-1, width)
        wide_col = col.astype(jnp.float32)
        squared = wide_col * wide_col
        folded = squared[:, :128]
        for k in range(128, width, 128):
            folded = folded + squared[:, k : k + 128]
        col_norm = -rate * jnp.sum(folded.T, axis=0, keepdims=True)
        inner = lax.dot_general(
            rows[where, :], col, (((1,), (1,)), ((), ())), preferred_element_type=jnp.float32
        )
        row_norm = norm[where, :]
        weights = []
        folded = None
        for k in range(0, col.shape[0], lanes):
            f = jnp.exp2(
                inner[:, k : k + lanes] * (2.0 * rate) + (row_norm + col_norm[:, k : k + lanes])
            )
            f2 = f * f
            f4 = f2 * f2
            f8 = f4 * f4
            summed = f * (LOW + f * (MID + f2 * (HIGH + f4 * (1.0 + f8))))
            weight = (summed * sign).astype(jnp.bfloat16)
            weights.append(weight)
            wide = weight.astype(jnp.float32)
            folded = wide if folded is None else folded + wide
        pulled = jnp.dot(
            jnp.concatenate(weights, axis=1), col, preferred_element_type=jnp.float32
        )
        return folded, pulled

    def use(read, first=False):
        folded, pulled = weigh(read, slice(0, rows.shape[0]))
        if first:
            mass[...] = folded
            acc[...] = pulled
        else:
            mass[...] += folded
            acc[...] += pulled

    def events(dist, i):
        ways = range(2)
        return [(slot_of(way, dist), way, (i + way) % 2) for way in ways]

    def arrive(dist, i):
        if dist == 1:
            for kind in range(2):
                for slot, way, part in events(dist, i):
                    z_first(way, part, kind).wait_recv()
                    send(x_copy(slot, part, kind))
        for slot, way, part in events(dist, i):
            if dist > 1:
                z_copy(way, dist, part).wait_recv()
                send(x_copy(slot, part))
            if dist + 1 < half_nz or (dist + 1 == half_nz and part == way):
                send(z_copy(way, dist + 1, part))
            send(mate_copy(slot, 0, part))

    def cross(dist, i):
        for slot, way, part in events(dist, i):
            x_copy(slot, part).wait_recv()
            send(mate_copy(slot, 1, 1 - part))

    def take(slots, half):
        for slot in slots:
            for part in range(2):
                mate_copy(slot, half, part).wait_recv()

    def use_pair(dist, half):
        slot = slot_of(0, dist)
        take((slot, slot + 1), half)
        use(lambda: cols[slot : slot + 2, half])

    arrive(1, 0)
    for part in range(2):
        x_copy(0, part).wait_recv()
        send(mate_copy(0, 1, 1 - part))
    arrive(1, 1)
    take((0,), 1)
    use(lambda: cols[0], first=True)
    cross(1, 0)
    for dist in range(2, half_nz):
        arrive(dist, 0)
        use_pair(dist - 1, 0)
        cross(dist - 1, 1)
        arrive(dist, 1)
        use_pair(dist - 1, 1)
        cross(dist, 0)
    arrive(half_nz, 0)
    use_pair(half_nz - 1, 0)
    cross(half_nz - 1, 1)
    take((last,), 0)
    use(lambda: cols[last, 0])
    cross(half_nz, 0)
    use_pair(half_nz - 1, 1)
    take((last,), 1)

    reduced = []
    batch = min(4, len(owners))
    for begin in range(0, len(owners), batch):
        where = slice(begin * share_rows, (begin + batch) * share_rows)
        folded, pulled = weigh(lambda: cols[last, 1], where)
        diff = jnp.sum(mass[where, :] + folded, axis=1, keepdims=True)
        total = acc[where, :] + pulled - diff * rows[where, :].astype(jnp.float32)
        for i in range(begin, begin + batch):
            share = total[(i - begin) * share_rows : (i - begin + 1) * share_rows]
            if owners[i] == (0, 0):
                acc[i * share_rows : (i + 1) * share_rows, :] = share
            else:
                stage[i] = share.astype(jnp.bfloat16)
                send(owner_copy(i), reduced)

    for copy in gathered:
        copy.wait_send()
    total = acc[(len(owners) - 1) * share_rows :, :]
    for i in range(len(owners) - 1):
        owner_copy(i).wait_recv()
        total = total + landed[i].astype(jnp.float32)
    out[...] = total * (1.0 / (groups * blks * share_rows))
    for copy in reduced:
        copy.wait_send()


def local(student, teacher):
    groups, blks = lax.axis_size("group"), lax.axis_size("blk")
    local_rows, width = student.shape
    nz, ny = groups // X_LO, blks // (X_HI * CORES)
    share_rows = local_rows // blks
    part_rows = local_rows // (ny * X * CORES)
    core_rows = local_rows // CORES
    dma = pltpu.SemaphoreType.DMA
    pairs = groups * local_rows * 2 * groups * local_rows // (groups * blks)
    return pl.pallas_call(
        functools.partial(kernel, groups=groups, blks=blks),
        out_shape=jax.ShapeDtypeStruct((share_rows, width), jnp.float32),
        in_specs=[pl.BlockSpec(memory_space=pltpu.HBM)] * 2,
        out_specs=pl.BlockSpec(memory_space=pltpu.VMEM),
        scratch_shapes=[
            pltpu.VMEM((core_rows, width), jnp.bfloat16),
            pltpu.VMEM((nz, 2, CORES, 2, 2, part_rows, width), jnp.bfloat16),
            pltpu.VMEM((core_rows, width), jnp.float32),
            pltpu.VMEM((core_rows, 128), jnp.float32),
            pltpu.VMEM((core_rows, 128), jnp.float32),
            pltpu.VMEM((ny * X_HI, share_rows, width), jnp.bfloat16),
            pltpu.VMEM((ny * X_HI, share_rows, width), jnp.bfloat16),
            dma((ny * X_HI,)),
            dma((CORES, 2, 2)),
            dma((2, 2, 2)),
            dma((2, 2, 2)),
            dma((3, 2, 2)),
            dma((2, nz // 2, 2)),
            dma((2, nz // 2, 2)),
            dma((nz, 2)),
            dma((nz, 2)),
            dma((nz, 2, 2)),
            dma((nz, 2, 2)),
            dma((ny * X_HI,)),
            dma((ny * X_HI,)),
        ],
        compiler_params=pltpu.CompilerParams(
            collective_id=0, has_side_effects=True, vmem_limit_bytes=52 * 1024 * 1024
        ),
        cost_estimate=pl.CostEstimate(
            flops=4 * pairs * width, bytes_accessed=8 * 1024 * 1024, transcendentals=pairs
        ),
    )(student, teacher)


def solution(mesh):
    in_specs = (P("group", None), P("group", None))
    out_specs = P(("group", "blk"), None)
    return jax.shard_map(local, mesh=mesh, in_specs=in_specs, out_specs=out_specs, check_vma=False)
```

```python
import functools
import math

import jax
import jax.numpy as jnp
from jax import lax
from jax.experimental import pallas as pl
from jax.experimental.pallas import tpu as pltpu
from jax.sharding import PartitionSpec as P

X_HI = 2
X_LO = 2
CORES = 2
X = X_HI * X_LO
WIDEST = 8.0

LOW = 0.25 * 2.0 ** -0.125
MID = 0.5 * 2.0 ** -0.25
HIGH = 2.0 ** -0.5


SCALE = 2.0**9


def encode(value):
    scaled = value * SCALE
    squared = scaled * scaled
    return (squared * scaled * jnp.abs(scaled)).astype(jnp.bfloat16)


def decode(code):
    wide = code.astype(jnp.float32)
    root = lax.rsqrt(lax.rsqrt(jnp.abs(wide))) * (1.0 / SCALE)
    return jnp.where(wide < 0.0, -root, root)


def kernel(student, teacher, out, cols, col_norm, rows, norm, mass, res, x_out, x_in, z_out, z_in, far_out, far_in,
           load_sem, own_sem, z_send, z_recv, x_send, x_recv,
           x_back_send, x_back_recv, z_back_send, z_back_recv, far_send, far_recv, *, groups, blks):
    nz = groups // X_LO
    width = cols.shape[1]
    part_rows = rows.shape[3]
    share_rows = 2 * part_rows
    local_rows = cols.shape[0] // 2
    half_nz = nz // 2
    last = nz - 1

    group = lax.axis_index("group")
    blk = lax.axis_index("blk")
    x_lo, z = group // nz, lax.rem(group, nz)
    y, x_hi, core = blk // (X_HI * CORES), lax.rem(blk // CORES, X_HI), lax.rem(blk, CORES)
    x = x_hi * X_LO + x_lo

    def at_z(step):
        return {"group": x_lo * nz + lax.rem(z + step + nz, nz), "blk": blk}

    def at_x(step):
        to = lax.rem(x + step + X, X)
        return {
            "group": lax.rem(to, X_LO) * nz + z,
            "blk": (y * X_HI + to // X_LO) * CORES + core,
        }

    def remote(src, dst, send_sem, recv_sem, to):
        return pltpu.make_async_remote_copy(
            src_ref=src,
            dst_ref=dst,
            send_sem=send_sem,
            recv_sem=recv_sem,
            device_id=to,
            device_id_type=pl.DeviceIdType.MESH,
        )

    def away(way):
        return 1 if way == 0 else -1

    def own_part(part):
        start = blk * share_rows + part * part_rows
        return student.at[pl.ds(pl.multiple_of(start, part_rows), part_rows)]

    def slot_of(way, dist):
        if dist == 0:
            return 0
        if dist == half_nz:
            return last
        return 2 * dist - 1 + way

    def z_copy(way, dist, part):
        at = (way, dist - 1, part)
        src = own_part(part) if dist == 1 else rows.at[slot_of(way, dist - 1), 0, part]
        return remote(
            src, rows.at[slot_of(way, dist), 0, part], z_send.at[at], z_recv.at[at], at_z(away(way))
        )

    def x_copy(slot, part):
        src = own_part(part) if slot == 0 else rows.at[slot, 0, part]
        at = (slot, part)
        return remote(
            src, rows.at[slot, 1, 1 - part], x_send.at[at], x_recv.at[at], at_x(-1 if part == 0 else 1)
        )

    def x_back(slot, index):
        at = (slot, index)
        return remote(
            x_out.at[at],
            x_in.at[slot, 1 - index],
            x_back_send.at[at],
            x_back_recv.at[slot, 1 - index],
            at_x(1 if index == 1 else -1),
        )

    def wait_x_back(slot, part):
        at = (slot, part)
        remote(
            x_out.at[at], x_in.at[at], x_back_send.at[at], x_back_recv.at[at], at_x(1)
        ).wait_recv()

    def z_back(way, dist, part):
        at = (way, dist - 1, part)
        return remote(
            z_out.at[at], z_in.at[at], z_back_send.at[at], z_back_recv.at[at], at_z(-away(way))
        )

    def far_back(part):
        return remote(
            far_out.at[part], far_in.at[part], far_send.at[part], far_recv.at[part], at_z(half_nz)
        )

    loads = [
        pltpu.make_async_copy(student, cols.at[pl.ds(0, local_rows)], load_sem.at[0]),
        pltpu.make_async_copy(teacher, cols.at[pl.ds(local_rows, local_rows)], load_sem.at[1]),
    ]
    loads += [
        pltpu.make_async_copy(own_part(part), rows.at[0, 0, part], own_sem.at[part])
        for part in range(2)
    ]
    barrier = pltpu.get_barrier_semaphore()
    partners = [at_z(1), at_z(-1), at_x(1), at_x(-1), at_z(half_nz)]
    for partner in partners:
        pl.semaphore_signal(barrier, inc=1, device_id=partner, device_id_type=pl.DeviceIdType.MESH)
    for copy in loads:
        copy.start()
    pl.semaphore_wait(barrier, len(partners))

    sent = []

    def send(copy):
        copy.start()
        sent.append(copy)

    for i in range(2):
        for way in range(2):
            send(z_copy(way, 1, (i + way) % 2))
        send(x_copy(0, i))

    rate = math.log2(math.e) / (WIDEST * width)
    for copy in loads:
        copy.wait()

    @pl.loop(0, 2 * local_rows // 256)
    def _(i):
        wide = cols[pl.ds(pl.multiple_of(i * 256, 256), 256), :].astype(jnp.float32)
        squared = wide * wide
        folded = squared[:, :128]
        for k in range(128, width, 128):
            folded = folded + squared[:, k : k + 128]
        col_norm[i, :, :] = jnp.broadcast_to(-rate * jnp.sum(folded.T, axis=0, keepdims=True), (8, 256))

    step = 512

    def weigh(row, row_norm, begin):
        col = cols[begin : begin + step, :]
        inner = lax.dot_general(
            row, col, (((1,), (1,)), ((), ())), preferred_element_type=jnp.float32
        )
        weights = []
        folded = None
        for k in range(0, step, 128):
            at = (begin + k) // 256
            norms = col_norm[at, 0:1, :][:, (begin + k) % 256 : (begin + k) % 256 + 128]
            f = jnp.exp2(inner[:, k : k + 128] * (2.0 * rate) + (row_norm + norms))
            f2 = f * f
            f4 = f2 * f2
            f8 = f4 * f4
            summed = f * (LOW + f * (MID + f2 * (HIGH + f4 * (1.0 + f8))))
            weight = (summed if begin < local_rows else -summed).astype(jnp.bfloat16)
            weights.append(weight)
            wide = weight.astype(jnp.float32)
            folded = wide if folded is None else folded + wide
        pulled = jnp.dot(
            jnp.concatenate(weights, axis=1), col, preferred_element_type=jnp.float32
        )
        return folded, pulled

    def use(slot, count, quarters=range(4)):
        row = rows[slot : slot + count].reshape(-1, width)
        where = slice(slot * 2 * share_rows, (slot + count) * 2 * share_rows)
        if 0 in quarters:
            wide = row.astype(jnp.float32)
            total = jnp.sum(wide * wide, axis=1, keepdims=True)
            norm[where, :] = jnp.broadcast_to(0.125 - rate * total, (row.shape[0], 128))
        for quarter in quarters:
            folded, pulled = weigh(row, norm[where, :], quarter * step)
            if quarter == 0:
                mass[where, :] = folded
                res[where, :] = pulled
            else:
                mass[where, :] += folded
                res[where, :] += pulled
        if 3 in quarters:
            diff = jnp.sum(mass[where, :], axis=1, keepdims=True)
            whole = res[where, :] - diff * row.astype(jnp.float32)
            res[where, :] = whole
            for c in range(count):
                for index in range(2):
                    start = (2 * c + 1) * share_rows + index * part_rows
                    x_out[slot + c, index] = encode(whole[start : start + part_rows])

    def own_sum(slot, part):
        wait_x_back(slot, part)
        start = slot * 2 * share_rows + part * part_rows
        return res[start : start + part_rows, :] + decode(x_in[slot, part])

    def keep(slot, part):
        start = slot * 2 * share_rows + part * part_rows
        res[start : start + part_rows, :] = own_sum(slot, part)

    def kept(slot, part):
        start = slot * 2 * share_rows + part * part_rows
        return res[start : start + part_rows, :]

    def arrive(dist, i):
        for way in range(2):
            part = (i + way) % 2
            z_copy(way, dist, part).wait_recv()
            if dist + 1 < half_nz or (dist + 1 == half_nz and part == way):
                send(z_copy(way, dist + 1, part))
            send(x_copy(slot_of(way, dist), part))

    def cross(*slots):
        for slot in slots:
            for part in range(2):
                x_copy(slot, part).wait_recv()

    def give_back(*slots):
        for slot in slots:
            for index in range(2):
                send(x_back(slot, index))

    arrive(1, 0)
    arrive(1, 1)
    cross(0)
    use(0, 1)
    for dist in range(2, half_nz):
        slot = slot_of(0, dist - 1)
        if dist == 2:
            arrive(2, 0)
            arrive(2, 1)
        cross(slot, slot + 1)
        use(slot, 2, range(2))
        if dist + 1 < half_nz:
            arrive(dist + 1, 0)
        else:
            arrive(half_nz, 0)
            give_back(0)
            for early in range(1, half_nz - 2):
                give_back(slot_of(0, early), slot_of(1, early))
        use(slot, 2, range(2, 4))
        if dist + 1 < half_nz:
            arrive(dist + 1, 1)
    slot = slot_of(0, half_nz - 2)
    give_back(slot, slot + 1)
    slot = slot_of(0, half_nz - 1)
    cross(slot, slot + 1)
    use(slot, 2)
    give_back(slot, slot + 1)
    cross(last)
    use(last, 1)
    give_back(last)

    for dist in range(half_nz - 1):
        for slot in sorted({slot_of(0, dist), slot_of(1, dist)}):
            for part in range(2):
                keep(slot, part)
    for part in range(2):
        for way in range(2):
            z_out[way, half_nz - 2, part] = encode(own_sum(slot_of(way, half_nz - 1), part))
            send(z_back(way, half_nz - 1, part))
    for part in range(2):
        far_out[part] = encode(own_sum(last, part))
        send(far_back(part))
    for dist in range(half_nz - 2, 0, -1):
        for part in range(2):
            for way in range(2):
                z_back(way, dist + 1, part).wait_recv()
                z_out[way, dist - 1, part] = encode(
                    kept(slot_of(way, dist), part) + decode(z_in[way, dist, part])
                )
                send(z_back(way, dist, part))
    for part in range(2):
        far_back(part).wait_recv()
        res[part * part_rows : (part + 1) * part_rows, :] = kept(0, part) + decode(far_in[part])
    for copy in sent:
        copy.wait_send()
    for part in range(2):
        total = kept(0, part)
        for way in range(2):
            z_back(way, 1, part).wait_recv()
            total = total + decode(z_in[way, 0, part])
        out[part * part_rows : (part + 1) * part_rows, :] = total * (1.0 / (groups * local_rows))


def local(student, teacher):
    groups, blks = lax.axis_size("group"), lax.axis_size("blk")
    local_rows, width = student.shape
    nz = groups // X_LO
    share_rows = local_rows // blks
    part_rows = share_rows // 2
    dist = nz // 2
    dma = pltpu.SemaphoreType.DMA
    pairs = groups * local_rows * 2 * groups * local_rows // (groups * blks)
    return pl.pallas_call(
        functools.partial(kernel, groups=groups, blks=blks),
        out_shape=jax.ShapeDtypeStruct((share_rows, width), jnp.float32),
        in_specs=[pl.BlockSpec(memory_space=pltpu.HBM)] * 2,
        out_specs=pl.BlockSpec(memory_space=pltpu.VMEM),
        scratch_shapes=[
            pltpu.VMEM((2 * local_rows, width), jnp.bfloat16),
            pltpu.VMEM((2 * local_rows // 256, 8, 256), jnp.float32),
            pltpu.VMEM((nz, 2, 2, part_rows, width), jnp.bfloat16),
            pltpu.VMEM((nz * 2 * share_rows, 128), jnp.float32),
            pltpu.VMEM((nz * 2 * share_rows, 128), jnp.float32),
            pltpu.VMEM((nz * 2 * share_rows, width), jnp.float32),
            pltpu.VMEM((nz, 2, part_rows, width), jnp.bfloat16),
            pltpu.VMEM((nz, 2, part_rows, width), jnp.bfloat16),
            pltpu.VMEM((2, dist - 1, 2, part_rows, width), jnp.bfloat16),
            pltpu.VMEM((2, dist - 1, 2, part_rows, width), jnp.bfloat16),
            pltpu.VMEM((2, part_rows, width), jnp.bfloat16),
            pltpu.VMEM((2, part_rows, width), jnp.bfloat16),
            dma((2,)),
            dma((2,)),
            dma((2, dist, 2)),
            dma((2, dist, 2)),
            dma((nz, 2)),
            dma((nz, 2)),
            dma((nz, 2)),
            dma((nz, 2)),
            dma((2, dist - 1, 2)),
            dma((2, dist - 1, 2)),
            dma((2,)),
            dma((2,)),
        ],
        compiler_params=pltpu.CompilerParams(
            collective_id=0, has_side_effects=True, vmem_limit_bytes=52 * 1024 * 1024
        ),
        cost_estimate=pl.CostEstimate(
            flops=4 * pairs * width, bytes_accessed=8 * 1024 * 1024, transcendentals=pairs
        ),
    )(student, teacher)


def solution(mesh):
    in_specs = (P("group", None), P("group", None))
    out_specs = P(("group", "blk"), None)
    return jax.shard_map(local, mesh=mesh, in_specs=in_specs, out_specs=out_specs, check_vma=False)
```

```python
import functools
import math

import jax
import jax.numpy as jnp
from jax import lax
from jax.experimental import pallas as pl
from jax.experimental.pallas import tpu as pltpu
from jax.sharding import PartitionSpec as P

X_HI = 2
X_LO = 2
CORES = 2
PARTS = 4
X = X_HI * X_LO
WIDEST = 8.0

LOW = 0.25 * 2.0 ** -0.125
MID = 0.5 * 2.0 ** -0.25
HIGH = 2.0 ** -0.5


SCALE = 2.0**9


def encode(value):
    scaled = value * SCALE
    squared = scaled * scaled
    return (squared * scaled * jnp.abs(scaled)).astype(jnp.bfloat16)


def decode(code):
    wide = code.astype(jnp.float32)
    root = lax.rsqrt(lax.rsqrt(jnp.abs(wide))) * (1.0 / SCALE)
    return jnp.where(wide < 0.0, -root, root)


def kernel(student, teacher, out, cols, col_norm, rows, norm, mass, res, x_out, x_in, z_out, z_in,
           load_sem, own_sem, z_send, z_recv, x_send, x_recv,
           x_back_send, x_back_recv, z_back_send, z_back_recv, *, groups, blks):
    nz = groups // X_LO
    width = cols.shape[1]
    part_rows = rows.shape[3]
    share_rows = PARTS * part_rows
    local_rows = cols.shape[0] // 2
    half_nz = nz // 2
    last = nz - 1

    group = lax.axis_index("group")
    blk = lax.axis_index("blk")
    x_lo, z = group // nz, lax.rem(group, nz)
    y, x_hi, core = blk // (X_HI * CORES), lax.rem(blk // CORES, X_HI), lax.rem(blk, CORES)
    x = x_hi * X_LO + x_lo

    def at_z(step):
        return {"group": x_lo * nz + lax.rem(z + step + nz, nz), "blk": blk}

    def at_x(step):
        to = lax.rem(x + step + X, X)
        return {
            "group": lax.rem(to, X_LO) * nz + z,
            "blk": (y * X_HI + to // X_LO) * CORES + core,
        }

    def remote(src, dst, send_sem, recv_sem, to):
        return pltpu.make_async_remote_copy(
            src_ref=src,
            dst_ref=dst,
            send_sem=send_sem,
            recv_sem=recv_sem,
            device_id=to,
            device_id_type=pl.DeviceIdType.MESH,
        )

    def away(way):
        return 1 if way == 0 else -1

    def own_part(part):
        start = blk * share_rows + part * part_rows
        return student.at[pl.ds(pl.multiple_of(start, part_rows), part_rows)]

    def slot_of(way, dist):
        if dist == 0:
            return 0
        if dist == half_nz:
            return last
        return 2 * dist - 1 + way

    def side(part):
        return part // (PARTS // 2)

    def flip(part):
        return (part + PARTS // 2) % PARTS

    order = [
        [(i % 2 ^ way) * (PARTS // 2) + i // 2 for i in range(PARTS)] for way in range(2)
    ]

    def z_copy(way, dist, part):
        at = (way, dist - 1, part)
        src = own_part(part) if dist == 1 else rows.at[slot_of(way, dist - 1), 0, part]
        return remote(
            src, rows.at[slot_of(way, dist), 0, part], z_send.at[at], z_recv.at[at], at_z(away(way))
        )

    def x_copy(slot, part):
        src = own_part(part) if slot == 0 else rows.at[slot, 0, part]
        at = (slot, part)
        return remote(
            src, rows.at[slot, 1, flip(part)], x_send.at[at], x_recv.at[at], at_x(-1 if side(part) == 0 else 1)
        )

    def x_back(slot, index):
        at = (slot, index)
        return remote(
            x_out.at[at],
            x_in.at[slot, flip(index)],
            x_back_send.at[at],
            x_back_recv.at[slot, flip(index)],
            at_x(1 if side(index) == 1 else -1),
        )

    def wait_x_back(slot, part):
        at = (slot, part)
        remote(
            x_out.at[at], x_in.at[at], x_back_send.at[at], x_back_recv.at[at], at_x(1)
        ).wait_recv()

    def z_back(way, dist, part):
        at = (way, dist - 1, part)
        return remote(
            z_out.at[at], z_in.at[at], z_back_send.at[at], z_back_recv.at[at], at_z(-away(way))
        )

    loads = [
        pltpu.make_async_copy(student, cols.at[pl.ds(0, local_rows)], load_sem.at[0]),
        pltpu.make_async_copy(teacher, cols.at[pl.ds(local_rows, local_rows)], load_sem.at[1]),
    ]
    loads += [
        pltpu.make_async_copy(own_part(part), rows.at[0, 0, part], own_sem.at[part])
        for part in range(PARTS)
    ]
    barrier = pltpu.get_barrier_semaphore()
    partners = [at_z(1), at_z(-1), at_x(1), at_x(-1)]
    for partner in partners:
        pl.semaphore_signal(barrier, inc=1, device_id=partner, device_id_type=pl.DeviceIdType.MESH)
    for copy in loads:
        copy.start()
    pl.semaphore_wait(barrier, len(partners))

    sent = []

    def send(copy):
        copy.start()
        sent.append(copy)

    for i in range(PARTS):
        for way in range(2):
            send(z_copy(way, 1, order[way][i]))
        send(x_copy(0, order[0][i]))

    rate = math.log2(math.e) / (WIDEST * width)
    for copy in loads:
        copy.wait()

    @pl.loop(0, 2 * local_rows // 256)
    def _(i):
        wide = cols[pl.ds(pl.multiple_of(i * 256, 256), 256), :].astype(jnp.float32)
        squared = wide * wide
        folded = squared[:, :128]
        for k in range(128, width, 128):
            folded = folded + squared[:, k : k + 128]
        col_norm[i, :, :] = jnp.broadcast_to(-rate * jnp.sum(folded.T, axis=0, keepdims=True), (8, 256))

    step = 512

    def weigh(row, row_norm, begin):
        col = cols[begin : begin + step, :]
        inner = lax.dot_general(
            row, col, (((1,), (1,)), ((), ())), preferred_element_type=jnp.float32
        )
        weights = []
        folded = None
        for k in range(0, step, 128):
            at = (begin + k) // 256
            norms = col_norm[at, 0:1, :][:, (begin + k) % 256 : (begin + k) % 256 + 128]
            f = jnp.exp2(inner[:, k : k + 128] * (2.0 * rate) + (row_norm + norms))
            f2 = f * f
            f4 = f2 * f2
            f8 = f4 * f4
            summed = f * (LOW + f * (MID + f2 * (HIGH + f4 * (1.0 + f8))))
            weight = (summed if begin < local_rows else -summed).astype(jnp.bfloat16)
            weights.append(weight)
            wide = weight.astype(jnp.float32)
            folded = wide if folded is None else folded + wide
        pulled = jnp.dot(
            jnp.concatenate(weights, axis=1), col, preferred_element_type=jnp.float32
        )
        return folded, pulled

    def use(slot, count, quarters=range(4), half=None):
        read = rows[slot : slot + count] if half is None else rows[slot, half]
        row = read.reshape(-1, width)
        start = (2 * slot + (half or 0)) * share_rows
        where = slice(start, start + row.shape[0])
        if 0 in quarters:
            wide = row.astype(jnp.float32)
            total = jnp.sum(wide * wide, axis=1, keepdims=True)
            norm[where, :] = jnp.broadcast_to(0.125 - rate * total, (row.shape[0], 128))
        for quarter in quarters:
            folded, pulled = weigh(row, norm[where, :], quarter * step)
            if quarter == 0:
                mass[where, :] = folded
                res[where, :] = pulled
            else:
                mass[where, :] += folded
                res[where, :] += pulled
        if 3 in quarters:
            diff = jnp.sum(mass[where, :], axis=1, keepdims=True)
            whole = res[where, :] - diff * row.astype(jnp.float32)
            res[where, :] = whole
            if half == 0:
                return
            for c in range(count):
                for index in range(PARTS):
                    begin = (2 * c + (half is None)) * share_rows + index * part_rows
                    x_out[slot + c, index] = encode(whole[begin : begin + part_rows])

    def own_sum(slot, part):
        wait_x_back(slot, part)
        start = slot * 2 * share_rows + part * part_rows
        return res[start : start + part_rows, :] + decode(x_in[slot, part])

    def keep(slot, part):
        start = slot * 2 * share_rows + part * part_rows
        res[start : start + part_rows, :] = own_sum(slot, part)

    def kept(slot, part):
        start = slot * 2 * share_rows + part * part_rows
        return res[start : start + part_rows, :]

    def arrive(dist, indices):
        for i in indices:
            for way in range(2):
                part = order[way][i]
                if dist == half_nz and side(part) != way:
                    continue
                z_copy(way, dist, part).wait_recv()
                if dist + 1 < half_nz or (dist + 1 == half_nz and side(part) == way):
                    send(z_copy(way, dist + 1, part))
                send(x_copy(slot_of(way, dist), part))

    def cross(*slots):
        for slot in slots:
            for part in range(PARTS):
                x_copy(slot, part).wait_recv()

    def give_back(*slots):
        for index in range(PARTS):
            for slot in slots:
                send(x_back(slot, index))

    everything, first, second = range(PARTS), range(PARTS // 2), range(PARTS // 2, PARTS)
    near, mid, far = (slot_of(0, dist) for dist in range(1, half_nz))
    arrive(1, everything)
    arrive(2, everything)
    cross(near, near + 1)
    use(near, 2, [0])
    arrive(3, first)
    use(near, 2, [1])
    arrive(3, second)
    cross(mid, mid + 1)
    use(mid, 2, [0])
    arrive(4, first)
    use(mid, 2, [1])
    arrive(4, second)
    cross(far, far + 1)
    use(far, 2)
    give_back(far, far + 1)
    cross(last)
    use(last, 1)
    give_back(last)
    cross(0)

    def hand_back(way, dist, part, total):
        z_out[way, dist - 1, part] = encode(total)
        send(z_back(way, dist, part))

    def both(parts):
        return [(way, part) for i in range(PARTS // 2) for way in range(2) for part in [parts(way)[i]]]

    ready = both(lambda way: [part for part in everything if side(part) != way])
    later = both(lambda way: [part for part in everything if side(part) == way])
    for way, part in ready:
        hand_back(way, half_nz - 1, part, own_sum(slot_of(way, half_nz - 1), part))
    for way, part in later:
        hand_back(way, half_nz, part, own_sum(last, part))
    use(mid, 2, [2, 3])
    give_back(mid, mid + 1)
    for way, part in later:
        keep(slot_of(way, half_nz - 1), part)
    for way, part in later:
        z_back(way, half_nz, part).wait_recv()
        total = kept(slot_of(way, half_nz - 1), part) + decode(z_in[way, half_nz - 1, part])
        hand_back(way, half_nz - 1, part, total)
    use(near, 2, [2, 3])
    give_back(near, near + 1)
    for dist in range(half_nz - 2, -1, -1):
        for way, part in ready + later if dist else [(0, part) for part in everything]:
            keep(slot_of(way, dist), part)
        if dist > 0:
            for way, part in ready + later:
                z_back(way, dist + 1, part).wait_recv()
                hand_back(way, dist, part, kept(slot_of(way, dist), part) + decode(z_in[way, dist, part]))
        if dist + 2 == half_nz:
            use(0, 1)
            give_back(0)
    for copy in sent:
        copy.wait_send()
    scale = 1.0 / (groups * local_rows)
    for pick in (ready, later):
        for way, part in pick:
            z_back(way, 1, part).wait_recv()
            res[part * part_rows : (part + 1) * part_rows, :] = kept(0, part) + decode(z_in[way, 0, part])
    out[...] = res[:share_rows, :] * scale


def local(student, teacher):
    groups, blks = lax.axis_size("group"), lax.axis_size("blk")
    local_rows, width = student.shape
    nz = groups // X_LO
    share_rows = local_rows // blks
    part_rows = share_rows // PARTS
    dist = nz // 2
    dma = pltpu.SemaphoreType.DMA
    pairs = groups * local_rows * 2 * groups * local_rows // (groups * blks)
    return pl.pallas_call(
        functools.partial(kernel, groups=groups, blks=blks),
        out_shape=jax.ShapeDtypeStruct((share_rows, width), jnp.float32),
        in_specs=[pl.BlockSpec(memory_space=pltpu.HBM)] * 2,
        out_specs=pl.BlockSpec(memory_space=pltpu.VMEM),
        scratch_shapes=[
            pltpu.VMEM((2 * local_rows, width), jnp.bfloat16),
            pltpu.VMEM((2 * local_rows // 256, 8, 256), jnp.float32),
            pltpu.VMEM((nz, 2, PARTS, part_rows, width), jnp.bfloat16),
            pltpu.VMEM((nz * 2 * share_rows, 128), jnp.float32),
            pltpu.VMEM((nz * 2 * share_rows, 128), jnp.float32),
            pltpu.VMEM((nz * 2 * share_rows, width), jnp.float32),
            pltpu.VMEM((nz, PARTS, part_rows, width), jnp.bfloat16),
            pltpu.VMEM((nz, PARTS, part_rows, width), jnp.bfloat16),
            pltpu.VMEM((2, dist, PARTS, part_rows, width), jnp.bfloat16),
            pltpu.VMEM((2, dist, PARTS, part_rows, width), jnp.bfloat16),
            dma((2,)),
            dma((PARTS,)),
            dma((2, dist, PARTS)),
            dma((2, dist, PARTS)),
            dma((nz, PARTS)),
            dma((nz, PARTS)),
            dma((nz, PARTS)),
            dma((nz, PARTS)),
            dma((2, dist, PARTS)),
            dma((2, dist, PARTS)),
        ],
        compiler_params=pltpu.CompilerParams(
            collective_id=0, has_side_effects=True, vmem_limit_bytes=52 * 1024 * 1024
        ),
        cost_estimate=pl.CostEstimate(
            flops=4 * pairs * width, bytes_accessed=8 * 1024 * 1024, transcendentals=pairs
        ),
    )(student, teacher)


def solution(mesh):
    in_specs = (P("group", None), P("group", None))
    out_specs = P(("group", "blk"), None)
    return jax.shard_map(local, mesh=mesh, in_specs=in_specs, out_specs=out_specs, check_vma=False)
```

```python
import functools
import math

import jax
import jax.numpy as jnp
from jax import lax
from jax.experimental import pallas as pl
from jax.experimental.pallas import tpu as pltpu
from jax.sharding import PartitionSpec as P

X_HI = 2
X_LO = 2
CORES = 2
PARTS = 4
X = X_HI * X_LO
WIDEST = 8.0

LOW = 0.25 * 2.0 ** -0.125
MID = 0.5 * 2.0 ** -0.25
HIGH = 2.0 ** -0.5


SCALE = 2.0**9


def encode(value):
    scaled = value * SCALE
    squared = scaled * scaled
    return (squared * scaled * jnp.abs(scaled)).astype(jnp.bfloat16)


def decode(code):
    wide = code.astype(jnp.float32)
    root = lax.rsqrt(lax.rsqrt(jnp.abs(wide))) * (1.0 / SCALE)
    return jnp.where(wide < 0.0, -root, root)


def kernel(student, teacher, out, cols, col_norm, rows, norm, mass, res, x_out, x_in, z_out, z_in,
           load_sem, own_sem, z_send, z_recv, x_send, x_recv,
           x_back_send, x_back_recv, z_back_send, z_back_recv, *, groups, blks):
    nz = groups // X_LO
    width = cols.shape[1]
    part_rows = rows.shape[3]
    share_rows = PARTS * part_rows
    local_rows = cols.shape[0] // 2
    half_nz = nz // 2
    last = nz - 1

    group = lax.axis_index("group")
    blk = lax.axis_index("blk")
    x_lo, z = group // nz, lax.rem(group, nz)
    y, x_hi, core = blk // (X_HI * CORES), lax.rem(blk // CORES, X_HI), lax.rem(blk, CORES)
    x = x_hi * X_LO + x_lo

    def at_z(step):
        return {"group": x_lo * nz + lax.rem(z + step + nz, nz), "blk": blk}

    def at_x(step):
        to = lax.rem(x + step + X, X)
        return {
            "group": lax.rem(to, X_LO) * nz + z,
            "blk": (y * X_HI + to // X_LO) * CORES + core,
        }

    def remote(src, dst, send_sem, recv_sem, to):
        return pltpu.make_async_remote_copy(
            src_ref=src,
            dst_ref=dst,
            send_sem=send_sem,
            recv_sem=recv_sem,
            device_id=to,
            device_id_type=pl.DeviceIdType.MESH,
        )

    def away(way):
        return 1 if way == 0 else -1

    def own_part(part):
        start = blk * share_rows + part * part_rows
        return student.at[pl.ds(pl.multiple_of(start, part_rows), part_rows)]

    def slot_of(way, dist):
        if dist == 0:
            return 0
        if dist == half_nz:
            return last
        return 2 * dist - 1 + way

    def side(part):
        return part // (PARTS // 2)

    def flip(part):
        return (part + PARTS // 2) % PARTS

    order = [[(way * (PARTS // 2) + i) % PARTS for i in range(PARTS)] for way in range(2)]

    def z_copy(way, dist, part):
        at = (way, dist - 1, part)
        src = own_part(part) if dist == 1 else rows.at[slot_of(way, dist - 1), 0, part]
        return remote(
            src, rows.at[slot_of(way, dist), 0, part], z_send.at[at], z_recv.at[at], at_z(away(way))
        )

    def x_copy(slot, part):
        src = own_part(part) if slot == 0 else rows.at[slot, 0, part]
        at = (slot, part)
        return remote(
            src, rows.at[slot, 1, flip(part)], x_send.at[at], x_recv.at[at], at_x(-1 if side(part) == 0 else 1)
        )

    def x_back(slot, index):
        at = (slot, index)
        return remote(
            x_out.at[at],
            x_in.at[slot, flip(index)],
            x_back_send.at[at],
            x_back_recv.at[slot, flip(index)],
            at_x(1 if side(index) == 1 else -1),
        )

    def wait_x_back(slot, part):
        at = (slot, part)
        remote(
            x_out.at[at], x_in.at[at], x_back_send.at[at], x_back_recv.at[at], at_x(1)
        ).wait_recv()

    def z_back(way, dist, part):
        at = (way, dist - 1, part)
        return remote(
            z_out.at[at], z_in.at[at], z_back_send.at[at], z_back_recv.at[at], at_z(-away(way))
        )

    loads = [
        pltpu.make_async_copy(student, cols.at[pl.ds(0, local_rows)], load_sem.at[0]),
        pltpu.make_async_copy(teacher, cols.at[pl.ds(local_rows, local_rows)], load_sem.at[1]),
    ]
    loads += [
        pltpu.make_async_copy(own_part(part), rows.at[0, 0, part], own_sem.at[part])
        for part in range(PARTS)
    ]
    barrier = pltpu.get_barrier_semaphore()
    partners = [at_z(1), at_z(-1), at_x(1), at_x(-1)]
    for partner in partners:
        pl.semaphore_signal(barrier, inc=1, device_id=partner, device_id_type=pl.DeviceIdType.MESH)
    for copy in loads:
        copy.start()
    pl.semaphore_wait(barrier, len(partners))

    sent = []

    def send(copy):
        copy.start()
        sent.append(copy)

    for i in range(PARTS):
        for way in range(2):
            send(z_copy(way, 1, order[way][i]))
        send(x_copy(0, (i % 2) * (PARTS // 2) + i // 2))

    rate = math.log2(math.e) / (WIDEST * width)
    for copy in loads:
        copy.wait()

    @pl.loop(0, 2 * local_rows // 256)
    def _(i):
        wide = cols[pl.ds(pl.multiple_of(i * 256, 256), 256), :].astype(jnp.float32)
        squared = wide * wide
        folded = squared[:, :128]
        for k in range(128, width, 128):
            folded = folded + squared[:, k : k + 128]
        col_norm[i, :, :] = jnp.broadcast_to(-rate * jnp.sum(folded.T, axis=0, keepdims=True), (8, 256))

    step = 512

    def weigh(row, row_norm, begin):
        col = cols[begin : begin + step, :]
        inner = lax.dot_general(
            row, col, (((1,), (1,)), ((), ())), preferred_element_type=jnp.float32
        )
        weights = []
        folded = None
        for k in range(0, step, 128):
            at = (begin + k) // 256
            norms = col_norm[at, 0:1, :][:, (begin + k) % 256 : (begin + k) % 256 + 128]
            f = jnp.exp2(inner[:, k : k + 128] * (2.0 * rate) + (row_norm + norms))
            f2 = f * f
            f4 = f2 * f2
            f8 = f4 * f4
            summed = f * (LOW + f * (MID + f2 * (HIGH + f4 * (1.0 + f8))))
            weight = (summed if begin < local_rows else -summed).astype(jnp.bfloat16)
            weights.append(weight)
            wide = weight.astype(jnp.float32)
            folded = wide if folded is None else folded + wide
        return folded, weights

    def use(slot, count, quarters=range(4), half=None):
        read = rows[slot : slot + count] if half is None else rows[slot, half]
        row = read.reshape(-1, width)
        start = (2 * slot + (half or 0)) * share_rows
        where = slice(start, start + row.shape[0])
        if 0 in quarters:
            wide = row.astype(jnp.float32)
            total = jnp.sum(wide * wide, axis=1, keepdims=True)
            norm[where, :] = jnp.broadcast_to(0.125 - rate * total, (row.shape[0], 128))
        folded, weights = None, []
        for quarter in quarters:
            more, weight = weigh(row, norm[where, :], quarter * step)
            folded = more if folded is None else folded + more
            weights += weight
        pulled = jnp.dot(
            jnp.concatenate(weights, axis=1),
            cols[quarters[0] * step : (quarters[-1] + 1) * step, :],
            preferred_element_type=jnp.float32,
        )
        if 0 in quarters:
            mass[where, :] = folded
            res[where, :] = pulled
        else:
            mass[where, :] += folded
            res[where, :] += pulled
        if 3 in quarters:
            diff = jnp.sum(mass[where, :], axis=1, keepdims=True)
            whole = res[where, :] - diff * row.astype(jnp.float32)
            res[where, :] = whole
            if half == 0:
                return
            for c in range(count):
                for index in range(PARTS):
                    begin = (2 * c + (half is None)) * share_rows + index * part_rows
                    x_out[slot + c, index] = encode(whole[begin : begin + part_rows])

    def own_sum(slot, part):
        wait_x_back(slot, part)
        start = slot * 2 * share_rows + part * part_rows
        return res[start : start + part_rows, :] + decode(x_in[slot, part])

    def keep(slot, part):
        start = slot * 2 * share_rows + part * part_rows
        res[start : start + part_rows, :] = own_sum(slot, part)

    def kept(slot, part):
        start = slot * 2 * share_rows + part * part_rows
        return res[start : start + part_rows, :]

    def arrive(dist, indices):
        for i in indices:
            for way in range(2):
                part = order[way][i]
                if dist == half_nz and side(part) != way:
                    continue
                z_copy(way, dist, part).wait_recv()
                if dist + 1 < half_nz or (dist + 1 == half_nz and side(part) == way):
                    send(z_copy(way, dist + 1, part))
                send(x_copy(slot_of(way, dist), part))

    def cross(*slots):
        for slot in slots:
            for part in range(PARTS):
                x_copy(slot, part).wait_recv()

    def give_back(*slots):
        for index in range(PARTS):
            for slot in slots:
                send(x_back(slot, index))

    everything, first, second = range(PARTS), range(PARTS // 2), range(PARTS // 2, PARTS)
    near, mid, far = (slot_of(0, dist) for dist in range(1, half_nz))
    arrive(1, everything)
    arrive(2, everything)
    cross(near, near + 1)
    use(near, 2, [0])
    arrive(3, first)
    use(near, 2, [1])
    arrive(3, second)
    cross(mid, mid + 1)
    use(mid, 2, [0])
    arrive(4, first)
    use(mid, 2, [1])
    cross(far, far + 1)
    use(far, 2)
    give_back(far, far + 1)
    cross(last)
    use(last, 1)
    give_back(last)
    cross(0)

    def hand_back(way, dist, part, total):
        z_out[way, dist - 1, part] = encode(total)
        send(z_back(way, dist, part))

    def both(parts):
        return [(way, part) for i in range(PARTS // 2) for way in range(2) for part in [parts(way)[i]]]

    ready = both(lambda way: [part for part in everything if side(part) != way])
    later = both(lambda way: [part for part in everything if side(part) == way])
    for way, part in ready:
        hand_back(way, half_nz - 1, part, own_sum(slot_of(way, half_nz - 1), part))
    for way, part in later:
        hand_back(way, half_nz, part, own_sum(last, part))
    use(mid, 2, [2, 3])
    give_back(mid, mid + 1)
    for way, part in later:
        keep(slot_of(way, half_nz - 1), part)
    for way, part in later:
        z_back(way, half_nz, part).wait_recv()
        total = kept(slot_of(way, half_nz - 1), part) + decode(z_in[way, half_nz - 1, part])
        hand_back(way, half_nz - 1, part, total)
    use(near, 2, [2, 3])
    give_back(near, near + 1)
    for dist in range(half_nz - 2, -1, -1):
        for way, part in ready + later if dist else [(0, part) for part in everything]:
            keep(slot_of(way, dist), part)
        if dist > 0:
            for way, part in ready + later:
                z_back(way, dist + 1, part).wait_recv()
                hand_back(way, dist, part, kept(slot_of(way, dist), part) + decode(z_in[way, dist, part]))
        if dist + 2 == half_nz:
            use(0, 1)
            give_back(0)
    for copy in sent:
        copy.wait_send()
    scale = 1.0 / (groups * local_rows)
    for pick in (ready, later):
        for way, part in pick:
            z_back(way, 1, part).wait_recv()
            res[part * part_rows : (part + 1) * part_rows, :] = kept(0, part) + decode(z_in[way, 0, part])
    out[...] = res[:share_rows, :] * scale


def local(student, teacher):
    groups, blks = lax.axis_size("group"), lax.axis_size("blk")
    local_rows, width = student.shape
    nz = groups // X_LO
    share_rows = local_rows // blks
    part_rows = share_rows // PARTS
    dist = nz // 2
    dma = pltpu.SemaphoreType.DMA
    pairs = groups * local_rows * 2 * groups * local_rows // (groups * blks)
    return pl.pallas_call(
        functools.partial(kernel, groups=groups, blks=blks),
        out_shape=jax.ShapeDtypeStruct((share_rows, width), jnp.float32),
        in_specs=[pl.BlockSpec(memory_space=pltpu.HBM)] * 2,
        out_specs=pl.BlockSpec(memory_space=pltpu.VMEM),
        scratch_shapes=[
            pltpu.VMEM((2 * local_rows, width), jnp.bfloat16),
            pltpu.VMEM((2 * local_rows // 256, 8, 256), jnp.float32),
            pltpu.VMEM((nz, 2, PARTS, part_rows, width), jnp.bfloat16),
            pltpu.VMEM((nz * 2 * share_rows, 128), jnp.float32),
            pltpu.VMEM((nz * 2 * share_rows, 128), jnp.float32),
            pltpu.VMEM((nz * 2 * share_rows, width), jnp.float32),
            pltpu.VMEM((nz, PARTS, part_rows, width), jnp.bfloat16),
            pltpu.VMEM((nz, PARTS, part_rows, width), jnp.bfloat16),
            pltpu.VMEM((2, dist, PARTS, part_rows, width), jnp.bfloat16),
            pltpu.VMEM((2, dist, PARTS, part_rows, width), jnp.bfloat16),
            dma((2,)),
            dma((PARTS,)),
            dma((2, dist, PARTS)),
            dma((2, dist, PARTS)),
            dma((nz, PARTS)),
            dma((nz, PARTS)),
            dma((nz, PARTS)),
            dma((nz, PARTS)),
            dma((2, dist, PARTS)),
            dma((2, dist, PARTS)),
        ],
        compiler_params=pltpu.CompilerParams(
            collective_id=0, has_side_effects=True, vmem_limit_bytes=52 * 1024 * 1024
        ),
        cost_estimate=pl.CostEstimate(
            flops=4 * pairs * width, bytes_accessed=8 * 1024 * 1024, transcendentals=pairs
        ),
    )(student, teacher)


def solution(mesh):
    in_specs = (P("group", None), P("group", None))
    out_specs = P(("group", "blk"), None)
    return jax.shard_map(local, mesh=mesh, in_specs=in_specs, out_specs=out_specs, check_vma=False)
```

```python
import functools
import math

import jax
import jax.numpy as jnp
from jax import lax
from jax.experimental import pallas as pl
from jax.experimental.pallas import tpu as pltpu
from jax.sharding import PartitionSpec as P

X_HI = 2
X_LO = 2
CORES = 2
PARTS = 4
X = X_HI * X_LO
WIDEST = 8.0

LOW = 0.25 * 2.0 ** -0.125
MID = 0.5 * 2.0 ** -0.25
HIGH = 2.0 ** -0.5


SCALE = 2.0**9


def encode(value):
    scaled = value * SCALE
    squared = scaled * scaled
    return (squared * scaled * jnp.abs(scaled)).astype(jnp.bfloat16)


def decode(code):
    wide = code.astype(jnp.float32)
    root = lax.rsqrt(lax.rsqrt(jnp.abs(wide))) * (1.0 / SCALE)
    return jnp.where(wide < 0.0, -root, root)


def kernel(student, teacher, out, cols, col_norm, rows, norm, mass, res, x_out, x_in, z_out, z_in,
           load_sem, own_sem, z_send, z_recv, x_send, x_recv,
           x_back_send, x_back_recv, z_back_send, z_back_recv, *, groups, blks):
    nz = groups // X_LO
    width = cols.shape[1]
    part_rows = rows.shape[3]
    share_rows = PARTS * part_rows
    local_rows = cols.shape[0] // 2
    half_nz = nz // 2
    last = nz - 1

    group = lax.axis_index("group")
    blk = lax.axis_index("blk")
    x_lo, z = group // nz, lax.rem(group, nz)
    y, x_hi, core = blk // (X_HI * CORES), lax.rem(blk // CORES, X_HI), lax.rem(blk, CORES)
    x = x_hi * X_LO + x_lo

    def at_z(step):
        return {"group": x_lo * nz + lax.rem(z + step + nz, nz), "blk": blk}

    def at_x(step, z_step=0):
        to = lax.rem(x + step + X, X)
        return {
            "group": lax.rem(to, X_LO) * nz + lax.rem(z + z_step + nz, nz),
            "blk": (y * X_HI + to // X_LO) * CORES + core,
        }

    def remote(src, dst, send_sem, recv_sem, to):
        return pltpu.make_async_remote_copy(
            src_ref=src,
            dst_ref=dst,
            send_sem=send_sem,
            recv_sem=recv_sem,
            device_id=to,
            device_id_type=pl.DeviceIdType.MESH,
        )

    def away(way):
        return 1 if way == 0 else -1

    def own_part(part):
        start = blk * share_rows + part * part_rows
        return student.at[pl.ds(pl.multiple_of(start, part_rows), part_rows)]

    def slot_of(way, dist):
        if dist == 0:
            return 0
        if dist == half_nz:
            return last
        return 2 * dist - 1 + way

    def side(part):
        return part // (PARTS // 2)

    def flip(part):
        return (part + PARTS // 2) % PARTS

    order = [[(way * (PARTS // 2) + i) % PARTS for i in range(PARTS)] for way in range(2)]

    def z_copy(way, dist, part):
        at = (way, dist - 1, part)
        src = own_part(part) if dist == 1 else rows.at[slot_of(way, dist - 1), 0, part]
        return remote(
            src, rows.at[slot_of(way, dist), 0, part], z_send.at[at], z_recv.at[at], at_z(away(way))
        )

    def x_copy(slot, part):
        src = own_part(part) if slot == 0 else rows.at[slot, 0, part]
        at = (slot, part)
        return remote(
            src, rows.at[slot, 1, flip(part)], x_send.at[at], x_recv.at[at], at_x(-1 if side(part) == 0 else 1)
        )

    def x_back(slot, index):
        at = (slot, index)
        way_home = 1 if side(index) == 1 else -1
        return remote(
            x_out.at[at],
            x_in.at[slot, flip(index)],
            x_back_send.at[at],
            x_back_recv.at[slot, flip(index)],
            at_x(way_home, -way_home if slot == last else 0),
        )

    def wait_x_back(slot, part):
        at = (slot, part)
        remote(
            x_out.at[at], x_in.at[at], x_back_send.at[at], x_back_recv.at[at], at_x(1)
        ).wait_recv()

    def z_back(way, dist, part):
        at = (way, dist - 1, part)
        return remote(
            z_out.at[at], z_in.at[at], z_back_send.at[at], z_back_recv.at[at], at_z(-away(way))
        )

    loads = [
        pltpu.make_async_copy(student, cols.at[pl.ds(0, local_rows)], load_sem.at[0]),
        pltpu.make_async_copy(teacher, cols.at[pl.ds(local_rows, local_rows)], load_sem.at[1]),
    ]
    loads += [
        pltpu.make_async_copy(own_part(part), rows.at[0, 0, part], own_sem.at[part])
        for part in range(PARTS)
    ]
    barrier = pltpu.get_barrier_semaphore()
    partners = [at_z(1), at_z(-1), at_x(1), at_x(-1)]
    for partner in partners:
        pl.semaphore_signal(barrier, inc=1, device_id=partner, device_id_type=pl.DeviceIdType.MESH)
    for copy in loads:
        copy.start()
    pl.semaphore_wait(barrier, len(partners))

    sent = []

    def send(copy):
        copy.start()
        sent.append(copy)

    for i in range(PARTS):
        for way in range(2):
            send(z_copy(way, 1, order[way][i]))
        send(x_copy(0, (i % 2) * (PARTS // 2) + i // 2))

    rate = math.log2(math.e) / (WIDEST * width)
    for copy in loads:
        copy.wait()

    @pl.loop(0, 2 * local_rows // 256)
    def _(i):
        wide = cols[pl.ds(pl.multiple_of(i * 256, 256), 256), :].astype(jnp.float32)
        squared = wide * wide
        folded = squared[:, :128]
        for k in range(128, width, 128):
            folded = folded + squared[:, k : k + 128]
        col_norm[i, :, :] = jnp.broadcast_to(-rate * jnp.sum(folded.T, axis=0, keepdims=True), (8, 256))

    step = 512

    def weigh(row, row_norm, begin):
        col = cols[begin : begin + step, :]
        inner = lax.dot_general(
            row, col, (((1,), (1,)), ((), ())), preferred_element_type=jnp.float32
        )
        weights = []
        folded = None
        for k in range(0, step, 128):
            at = (begin + k) // 256
            norms = col_norm[at, 0:1, :][:, (begin + k) % 256 : (begin + k) % 256 + 128]
            f = jnp.exp2(inner[:, k : k + 128] * (2.0 * rate) + (row_norm + norms))
            f2 = f * f
            f4 = f2 * f2
            f8 = f4 * f4
            summed = f * (LOW + f * (MID + f2 * (HIGH + f4 * (1.0 + f8))))
            weight = (summed if begin < local_rows else -summed).astype(jnp.bfloat16)
            weights.append(weight)
            wide = weight.astype(jnp.float32)
            folded = wide if folded is None else folded + wide
        return folded, weights

    def use(slot, count, quarters=range(4), half=None):
        read = rows[slot : slot + count] if half is None else rows[slot, half]
        row = read.reshape(-1, width)
        start = (2 * slot + (half or 0)) * share_rows
        where = slice(start, start + row.shape[0])
        if 0 in quarters:
            wide = row.astype(jnp.float32)
            total = jnp.sum(wide * wide, axis=1, keepdims=True)
            norm[where, :] = jnp.broadcast_to(0.125 - rate * total, (row.shape[0], 128))
        folded, weights = None, []
        for quarter in quarters:
            more, weight = weigh(row, norm[where, :], quarter * step)
            folded = more if folded is None else folded + more
            weights += weight
        pulled = jnp.dot(
            jnp.concatenate(weights, axis=1),
            cols[quarters[0] * step : (quarters[-1] + 1) * step, :],
            preferred_element_type=jnp.float32,
        )
        if 0 in quarters:
            mass[where, :] = folded
            res[where, :] = pulled
        else:
            mass[where, :] += folded
            res[where, :] += pulled
        if 3 in quarters:
            diff = jnp.sum(mass[where, :], axis=1, keepdims=True)
            whole = res[where, :] - diff * row.astype(jnp.float32)
            res[where, :] = whole
            if half == 0:
                return
            for c in range(count):
                for index in range(PARTS):
                    begin = (2 * c + (half is None)) * share_rows + index * part_rows
                    x_out[slot + c, index] = encode(whole[begin : begin + part_rows])

    def own_sum(slot, part):
        wait_x_back(slot, part)
        start = slot * 2 * share_rows + part * part_rows
        return res[start : start + part_rows, :] + decode(x_in[slot, part])

    def keep(slot, part):
        start = slot * 2 * share_rows + part * part_rows
        res[start : start + part_rows, :] = own_sum(slot, part)

    def kept(slot, part):
        start = slot * 2 * share_rows + part * part_rows
        return res[start : start + part_rows, :]

    def arrive(dist, indices):
        for i in indices:
            for way in range(2):
                part = order[way][i]
                if dist == half_nz and side(part) != way:
                    continue
                z_copy(way, dist, part).wait_recv()
                if dist + 1 < half_nz or (dist + 1 == half_nz and side(part) == way):
                    send(z_copy(way, dist + 1, part))
                send(x_copy(slot_of(way, dist), part))

    def cross(*slots):
        for slot in slots:
            for part in range(PARTS):
                x_copy(slot, part).wait_recv()

    def give_back(*slots):
        for index in range(PARTS):
            for slot in slots:
                send(x_back(slot, index))

    everything, first, second = range(PARTS), range(PARTS // 2), range(PARTS // 2, PARTS)
    near, mid, far = (slot_of(0, dist) for dist in range(1, half_nz))
    arrive(1, everything)
    arrive(2, everything)
    cross(near, near + 1)
    use(near, 2, [0])
    arrive(3, first)
    use(near, 2, [1])
    arrive(3, second)
    cross(mid, mid + 1)
    use(mid, 2, [0])
    arrive(4, first)
    use(mid, 2, [1, 2, 3])
    give_back(mid, mid + 1)
    cross(far, far + 1)
    use(far, 2)
    give_back(far, far + 1)
    cross(last)
    use(last, 1)
    give_back(last)
    cross(0)

    def hand_back(way, dist, part, total):
        z_out[way, dist - 1, part] = encode(total)
        send(z_back(way, dist, part))

    def both(parts):
        return [(way, part) for i in range(PARTS // 2) for way in range(2) for part in [parts(way)[i]]]

    ready = both(lambda way: [part for part in everything if side(part) != way])
    later = both(lambda way: [part for part in everything if side(part) == way])
    for way, part in later:
        hand_back(way, half_nz, part, kept(last, part))
    for way, part in ready:
        hand_back(way, half_nz - 1, part, own_sum(slot_of(way, half_nz - 1), part))
    for way, part in later:
        keep(slot_of(way, half_nz - 1), part)
    for way, part in later:
        z_back(way, half_nz, part).wait_recv()
        wait_x_back(last, part)
        total = kept(slot_of(way, half_nz - 1), part) + decode(x_in[last, part])
        total = total + decode(z_in[way, half_nz - 1, part])
        hand_back(way, half_nz - 1, part, total)
    use(near, 2, [2, 3])
    give_back(near, near + 1)
    for dist in range(half_nz - 2, -1, -1):
        for way, part in ready + later if dist else [(0, part) for part in everything]:
            keep(slot_of(way, dist), part)
        if dist > 0:
            for way, part in ready + later:
                z_back(way, dist + 1, part).wait_recv()
                hand_back(way, dist, part, kept(slot_of(way, dist), part) + decode(z_in[way, dist, part]))
        if dist + 2 == half_nz:
            use(0, 1)
            give_back(0)
    for copy in sent:
        copy.wait_send()
    scale = 1.0 / (groups * local_rows)
    for pick in (ready, later):
        for way, part in pick:
            z_back(way, 1, part).wait_recv()
            res[part * part_rows : (part + 1) * part_rows, :] = kept(0, part) + decode(z_in[way, 0, part])
    out[...] = res[:share_rows, :] * scale


def local(student, teacher):
    groups, blks = lax.axis_size("group"), lax.axis_size("blk")
    local_rows, width = student.shape
    nz = groups // X_LO
    share_rows = local_rows // blks
    part_rows = share_rows // PARTS
    dist = nz // 2
    dma = pltpu.SemaphoreType.DMA
    pairs = groups * local_rows * 2 * groups * local_rows // (groups * blks)
    return pl.pallas_call(
        functools.partial(kernel, groups=groups, blks=blks),
        out_shape=jax.ShapeDtypeStruct((share_rows, width), jnp.float32),
        in_specs=[pl.BlockSpec(memory_space=pltpu.HBM)] * 2,
        out_specs=pl.BlockSpec(memory_space=pltpu.VMEM),
        scratch_shapes=[
            pltpu.VMEM((2 * local_rows, width), jnp.bfloat16),
            pltpu.VMEM((2 * local_rows // 256, 8, 256), jnp.float32),
            pltpu.VMEM((nz, 2, PARTS, part_rows, width), jnp.bfloat16),
            pltpu.VMEM((nz * 2 * share_rows, 128), jnp.float32),
            pltpu.VMEM((nz * 2 * share_rows, 128), jnp.float32),
            pltpu.VMEM((nz * 2 * share_rows, width), jnp.float32),
            pltpu.VMEM((nz, PARTS, part_rows, width), jnp.bfloat16),
            pltpu.VMEM((nz, PARTS, part_rows, width), jnp.bfloat16),
            pltpu.VMEM((2, dist, PARTS, part_rows, width), jnp.bfloat16),
            pltpu.VMEM((2, dist, PARTS, part_rows, width), jnp.bfloat16),
            dma((2,)),
            dma((PARTS,)),
            dma((2, dist, PARTS)),
            dma((2, dist, PARTS)),
            dma((nz, PARTS)),
            dma((nz, PARTS)),
            dma((nz, PARTS)),
            dma((nz, PARTS)),
            dma((2, dist, PARTS)),
            dma((2, dist, PARTS)),
        ],
        compiler_params=pltpu.CompilerParams(
            collective_id=0, has_side_effects=True, vmem_limit_bytes=52 * 1024 * 1024
        ),
        cost_estimate=pl.CostEstimate(
            flops=4 * pairs * width, bytes_accessed=8 * 1024 * 1024, transcendentals=pairs
        ),
    )(student, teacher)


def solution(mesh):
    in_specs = (P("group", None), P("group", None))
    out_specs = P(("group", "blk"), None)
    return jax.shard_map(local, mesh=mesh, in_specs=in_specs, out_specs=out_specs, check_vma=False)
```

```python
import functools
import math

import jax
import jax.numpy as jnp
from jax import lax
from jax.experimental import pallas as pl
from jax.experimental.pallas import tpu as pltpu
from jax.sharding import PartitionSpec as P

X_HI = 2
X_LO = 2
CORES = 2
PARTS = 4
X = X_HI * X_LO
WIDEST = 8.0

LOW = 0.25 * 2.0 ** -0.125
MID = 0.5 * 2.0 ** -0.25
HIGH = 2.0 ** -0.5


SCALE = 2.0**9


def encode(value):
    scaled = value * SCALE
    squared = scaled * scaled
    return (squared * scaled * jnp.abs(scaled)).astype(jnp.bfloat16)


def decode(code):
    wide = code.astype(jnp.float32)
    root = lax.rsqrt(lax.rsqrt(jnp.abs(wide))) * (1.0 / SCALE)
    return jnp.where(wide < 0.0, -root, root)


def kernel(student, teacher, out, cols, col_norm, rows, norm, mass, res, x_out, x_in, z_out, z_in,
           load_sem, own_sem, z_send, z_recv, x_send, x_recv,
           x_back_send, x_back_recv, z_back_send, z_back_recv, *, groups, blks):
    nz = groups // X_LO
    width = cols.shape[1]
    part_rows = rows.shape[3]
    share_rows = PARTS * part_rows
    local_rows = cols.shape[0] // 2
    half_nz = nz // 2
    last = nz - 1

    group = lax.axis_index("group")
    blk = lax.axis_index("blk")
    x_lo, z = group // nz, lax.rem(group, nz)
    y, x_hi, core = blk // (X_HI * CORES), lax.rem(blk // CORES, X_HI), lax.rem(blk, CORES)
    x = x_hi * X_LO + x_lo

    def at_z(step):
        return {"group": x_lo * nz + lax.rem(z + step + nz, nz), "blk": blk}

    def at_x(step, z_step=0):
        to = lax.rem(x + step + X, X)
        return {
            "group": lax.rem(to, X_LO) * nz + lax.rem(z + z_step + nz, nz),
            "blk": (y * X_HI + to // X_LO) * CORES + core,
        }

    def remote(src, dst, send_sem, recv_sem, to):
        return pltpu.make_async_remote_copy(
            src_ref=src,
            dst_ref=dst,
            send_sem=send_sem,
            recv_sem=recv_sem,
            device_id=to,
            device_id_type=pl.DeviceIdType.MESH,
        )

    def away(way):
        return 1 if way == 0 else -1

    def own_part(part):
        start = blk * share_rows + part * part_rows
        return student.at[pl.ds(pl.multiple_of(start, part_rows), part_rows)]

    def slot_of(way, dist):
        if dist == 0:
            return 0
        if dist == half_nz:
            return last
        return 2 * dist - 1 + way

    def side(part):
        return part // (PARTS // 2)

    def flip(part):
        return (part + PARTS // 2) % PARTS

    order = [[(way * (PARTS // 2) + i) % PARTS for i in range(PARTS)] for way in range(2)]

    def z_copy(way, dist, part):
        at = (way, dist - 1, part)
        src = own_part(part) if dist == 1 else rows.at[slot_of(way, dist - 1), 0, part]
        return remote(
            src, rows.at[slot_of(way, dist), 0, part], z_send.at[at], z_recv.at[at], at_z(away(way))
        )

    def x_copy(slot, part):
        src = own_part(part) if slot == 0 else rows.at[slot, 0, part]
        at = (slot, part)
        return remote(
            src, rows.at[slot, 1, flip(part)], x_send.at[at], x_recv.at[at], at_x(-1 if side(part) == 0 else 1)
        )

    def x_back(slot, index):
        at = (slot, index)
        way_home = 1 if side(index) == 1 else -1
        return remote(
            x_out.at[at],
            x_in.at[slot, flip(index)],
            x_back_send.at[at],
            x_back_recv.at[slot, flip(index)],
            at_x(way_home, -way_home if slot == last else 0),
        )

    def wait_x_back(slot, part):
        at = (slot, part)
        remote(
            x_out.at[at], x_in.at[at], x_back_send.at[at], x_back_recv.at[at], at_x(1)
        ).wait_recv()

    def z_back(way, dist, part):
        at = (way, dist - 1, part)
        return remote(
            z_out.at[at], z_in.at[at], z_back_send.at[at], z_back_recv.at[at], at_z(-away(way))
        )

    loads = [
        pltpu.make_async_copy(student, cols.at[pl.ds(0, local_rows)], load_sem.at[0]),
        pltpu.make_async_copy(teacher, cols.at[pl.ds(local_rows, local_rows)], load_sem.at[1]),
    ]
    loads += [
        pltpu.make_async_copy(own_part(part), rows.at[0, 0, part], own_sem.at[part])
        for part in range(PARTS)
    ]
    barrier = pltpu.get_barrier_semaphore()
    partners = [at_z(1), at_z(-1), at_x(1), at_x(-1)]
    for partner in partners:
        pl.semaphore_signal(barrier, inc=1, device_id=partner, device_id_type=pl.DeviceIdType.MESH)
    for copy in loads:
        copy.start()
    pl.semaphore_wait(barrier, len(partners))

    sent = []

    def send(copy):
        copy.start()
        sent.append(copy)

    for i in range(PARTS):
        for way in range(2):
            send(z_copy(way, 1, order[way][i]))
        send(x_copy(0, (i % 2) * (PARTS // 2) + i // 2))

    rate = math.log2(math.e) / (WIDEST * width)
    for copy in loads:
        copy.wait()

    @pl.loop(0, 2 * local_rows // 256)
    def _(i):
        wide = cols[pl.ds(pl.multiple_of(i * 256, 256), 256), :].astype(jnp.float32)
        squared = wide * wide
        folded = squared[:, :128]
        for k in range(128, width, 128):
            folded = folded + squared[:, k : k + 128]
        col_norm[i, :, :] = jnp.broadcast_to(-rate * jnp.sum(folded.T, axis=0, keepdims=True), (8, 256))

    step = 512

    def weigh(row, row_norm, begin):
        col = cols[begin : begin + step, :]
        inner = lax.dot_general(
            row, col, (((1,), (1,)), ((), ())), preferred_element_type=jnp.float32
        )
        weights = []
        folded = None
        for k in range(0, step, 128):
            at = (begin + k) // 256
            norms = col_norm[at, 0:1, :][:, (begin + k) % 256 : (begin + k) % 256 + 128]
            f = jnp.exp2(inner[:, k : k + 128] * (2.0 * rate) + (row_norm + norms))
            f2 = f * f
            f4 = f2 * f2
            f8 = f4 * f4
            summed = f * (LOW + f * (MID + f2 * (HIGH + f4 * (1.0 + f8))))
            weight = (summed if begin < local_rows else -summed).astype(jnp.bfloat16)
            weights.append(weight)
            wide = weight.astype(jnp.float32)
            folded = wide if folded is None else folded + wide
        return folded, weights

    def use(slot, count, quarters=range(4), half=None):
        read = rows[slot : slot + count] if half is None else rows[slot, half]
        row = read.reshape(-1, width)
        start = (2 * slot + (half or 0)) * share_rows
        where = slice(start, start + row.shape[0])
        if 0 in quarters:
            wide = row.astype(jnp.float32)
            total = jnp.sum(wide * wide, axis=1, keepdims=True)
            norm[where, :] = jnp.broadcast_to(0.125 - rate * total, (row.shape[0], 128))
        folded, weights = None, []
        for quarter in quarters:
            more, weight = weigh(row, norm[where, :], quarter * step)
            folded = more if folded is None else folded + more
            weights += weight
        pulled = jnp.dot(
            jnp.concatenate(weights, axis=1),
            cols[quarters[0] * step : (quarters[-1] + 1) * step, :],
            preferred_element_type=jnp.float32,
        )
        if 0 in quarters:
            mass[where, :] = folded
            res[where, :] = pulled
        else:
            mass[where, :] += folded
            res[where, :] += pulled
        if 3 in quarters:
            diff = jnp.sum(mass[where, :], axis=1, keepdims=True)
            whole = res[where, :] - diff * row.astype(jnp.float32)
            res[where, :] = whole
            if half == 0:
                return
            for c in range(count):
                for index in range(PARTS):
                    begin = (2 * c + (half is None)) * share_rows + index * part_rows
                    x_out[slot + c, index] = encode(whole[begin : begin + part_rows])

    def own_sum(slot, part):
        wait_x_back(slot, part)
        start = slot * 2 * share_rows + part * part_rows
        return res[start : start + part_rows, :] + decode(x_in[slot, part])

    def keep(slot, part):
        start = slot * 2 * share_rows + part * part_rows
        res[start : start + part_rows, :] = own_sum(slot, part)

    def kept(slot, part):
        start = slot * 2 * share_rows + part * part_rows
        return res[start : start + part_rows, :]

    def arrive(dist, indices):
        for i in indices:
            for way in range(2):
                part = order[way][i]
                if dist == half_nz and side(part) != way:
                    continue
                z_copy(way, dist, part).wait_recv()
                if dist + 1 < half_nz or (dist + 1 == half_nz and side(part) == way):
                    send(z_copy(way, dist + 1, part))
                send(x_copy(slot_of(way, dist), part))

    def cross(*slots):
        for slot in slots:
            for part in range(PARTS):
                x_copy(slot, part).wait_recv()

    def give_back(*slots):
        for index in range(PARTS):
            for slot in slots:
                send(x_back(slot, index))

    everything, first, second = range(PARTS), range(PARTS // 2), range(PARTS // 2, PARTS)
    near, mid, far = (slot_of(0, dist) for dist in range(1, half_nz))
    arrive(1, everything)
    arrive(2, everything)
    cross(near, near + 1)
    use(near, 2, [0])
    arrive(3, first)
    use(near, 2, [1])
    arrive(3, second)
    cross(mid, mid + 1)
    use(mid, 2, [0])
    arrive(4, first)
    use(mid, 2, [1])
    cross(far, far + 1)
    use(far, 2)
    give_back(far, far + 1)
    cross(last)
    use(last, 1)
    give_back(last)
    cross(0)

    def hand_back(way, dist, part, total):
        z_out[way, dist - 1, part] = encode(total)
        send(z_back(way, dist, part))

    def both(parts):
        return [(way, part) for i in range(PARTS // 2) for way in range(2) for part in [parts(way)[i]]]

    ready = both(lambda way: [part for part in everything if side(part) != way])
    later = both(lambda way: [part for part in everything if side(part) == way])
    for way, part in later:
        hand_back(way, half_nz, part, kept(last, part))
    for way, part in ready:
        hand_back(way, half_nz - 1, part, own_sum(slot_of(way, half_nz - 1), part))
    use(mid, 2, [2, 3])
    give_back(mid, mid + 1)
    for way, part in later:
        keep(slot_of(way, half_nz - 1), part)
    for way, part in later:
        z_back(way, half_nz, part).wait_recv()
        wait_x_back(last, part)
        total = kept(slot_of(way, half_nz - 1), part) + decode(x_in[last, part])
        total = total + decode(z_in[way, half_nz - 1, part])
        hand_back(way, half_nz - 1, part, total)
    use(near, 2, [2, 3])
    give_back(near, near + 1)
    for dist in range(half_nz - 2, -1, -1):
        for way, part in ready + later if dist else [(0, part) for part in everything]:
            keep(slot_of(way, dist), part)
        if dist > 0:
            for way, part in ready + later:
                z_back(way, dist + 1, part).wait_recv()
                hand_back(way, dist, part, kept(slot_of(way, dist), part) + decode(z_in[way, dist, part]))
        if dist + 2 == half_nz:
            use(0, 1)
            give_back(0)
    for copy in sent:
        copy.wait_send()
    scale = 1.0 / (groups * local_rows)
    for pick in (ready, later):
        for way, part in pick:
            z_back(way, 1, part).wait_recv()
            res[part * part_rows : (part + 1) * part_rows, :] = kept(0, part) + decode(z_in[way, 0, part])
    out[...] = res[:share_rows, :] * scale


def local(student, teacher):
    groups, blks = lax.axis_size("group"), lax.axis_size("blk")
    local_rows, width = student.shape
    nz = groups // X_LO
    share_rows = local_rows // blks
    part_rows = share_rows // PARTS
    dist = nz // 2
    dma = pltpu.SemaphoreType.DMA
    pairs = groups * local_rows * 2 * groups * local_rows // (groups * blks)
    return pl.pallas_call(
        functools.partial(kernel, groups=groups, blks=blks),
        out_shape=jax.ShapeDtypeStruct((share_rows, width), jnp.float32),
        in_specs=[pl.BlockSpec(memory_space=pltpu.HBM)] * 2,
        out_specs=pl.BlockSpec(memory_space=pltpu.VMEM),
        scratch_shapes=[
            pltpu.VMEM((2 * local_rows, width), jnp.bfloat16),
            pltpu.VMEM((2 * local_rows // 256, 8, 256), jnp.float32),
            pltpu.VMEM((nz, 2, PARTS, part_rows, width), jnp.bfloat16),
            pltpu.VMEM((nz * 2 * share_rows, 128), jnp.float32),
            pltpu.VMEM((nz * 2 * share_rows, 128), jnp.float32),
            pltpu.VMEM((nz * 2 * share_rows, width), jnp.float32),
            pltpu.VMEM((nz, PARTS, part_rows, width), jnp.bfloat16),
            pltpu.VMEM((nz, PARTS, part_rows, width), jnp.bfloat16),
            pltpu.VMEM((2, dist, PARTS, part_rows, width), jnp.bfloat16),
            pltpu.VMEM((2, dist, PARTS, part_rows, width), jnp.bfloat16),
            dma((2,)),
            dma((PARTS,)),
            dma((2, dist, PARTS)),
            dma((2, dist, PARTS)),
            dma((nz, PARTS)),
            dma((nz, PARTS)),
            dma((nz, PARTS)),
            dma((nz, PARTS)),
            dma((2, dist, PARTS)),
            dma((2, dist, PARTS)),
        ],
        compiler_params=pltpu.CompilerParams(
            collective_id=0, has_side_effects=True, vmem_limit_bytes=52 * 1024 * 1024
        ),
        cost_estimate=pl.CostEstimate(
            flops=4 * pairs * width, bytes_accessed=8 * 1024 * 1024, transcendentals=pairs
        ),
    )(student, teacher)


def solution(mesh):
    in_specs = (P("group", None), P("group", None))
    out_specs = P(("group", "blk"), None)
    return jax.shard_map(local, mesh=mesh, in_specs=in_specs, out_specs=out_specs, check_vma=False)
```
